512 devices in a mesh: surf: 32 (over x, y, core), norm: 16 (over z).
Axes of the slice: x: 4, y: 4, z: 16, core: 2. Of those that a mesh axis runs over, the one named last changes fastest.
Arguments:
- mode_shapes: bfloat16 [128, 256, 3, 256], P('surf'), may hold values from -6 to 6
- amplitude: float32 [128], replicated, may hold values from -0.01171875 to 0.01171875
- mode_patch: int32 [128], replicated, may hold values from 0 to 3
- column_patch: int32 [256, 256], replicated, may hold values from 0 to 3
- wall_mask: int32 [256, 256], P('surf'), may hold values 0 or 1
- offsets: int32 [256, 256], P('surf'), may hold values from 0 to 511
- coupling: float32 [256, 256, 256], P('norm', 'surf'), may hold values from 0.5 to 2
- pivot_inv: float32 [256, 256, 9, 256], P('norm', 'surf'), may hold values from -2 to 2
- stiffness: float32 [256, 256, 256], P('norm', 'surf'), may hold values from 1.373291e-05 to 3.2043456e-05
Outputs:
- displacement: float32 [256, 256, 3, 256], P('norm', 'surf')
The draws below stay inside these ranges and needn't reach their ends.
All inputs are finite; a program needn't handle non-finite values. No bound on the sum of `wall_mask` on one device may be relied on, other than what follows from the above.
Results may differ from the reference program's by a relative error of at most 0.0006.
Values may be sent and summed in bfloat16 or wider, within the bound.
No kernel may reach another device: no remote copies, remote signals or barrier semaphores. Data moves between devices by JAX's collectives and lax.ppermute only.
A program may use at most 64 MiB of HBM per device.

```python
import math
import jax
import jax.numpy as jnp
from jax import lax

MODES = 128
PATCHES = 4
SWEEPS = 3
SPAN_COUNT_B = 256
SPAN_COUNT_A = 256
DEPTH_COUNT = 256


def coupling_values(key):
    return jnp.exp(jax.random.uniform(key, (DEPTH_COUNT, SPAN_COUNT_A, SPAN_COUNT_B), jnp.float32, math.log(0.5), math.log(2.0)))


def draw_coupling(key, part):
    return coupling_values(jax.random.fold_in(key, 11))


def euler_rotation(angle_a, angle_b, angle_g):
    cos_a, sin_a = (jnp.cos(angle_a), jnp.sin(angle_a))
    cos_b, sin_b = (jnp.cos(angle_b), jnp.sin(angle_b))
    cos_g, sin_g = (jnp.cos(angle_g), jnp.sin(angle_g))
    return [[cos_a * cos_b * cos_g - sin_a * sin_g, -cos_a * cos_b * sin_g - sin_a * cos_g, cos_a * sin_b], [sin_a * cos_b * cos_g + cos_a * sin_g, -sin_a * cos_b * sin_g + cos_a * cos_g, sin_a * sin_b], [-sin_b * cos_g, sin_b * sin_g, cos_b]]


def draw_pivot_inv(key, part):
    links = coupling_values(jax.random.fold_in(key, 11))
    generator_seeds = jax.random.split(jax.random.fold_in(key, 23), 6)
    slow_share = 0.5
    slow_flag = jax.random.uniform(generator_seeds[0], (SPAN_COUNT_A, 3, SPAN_COUNT_B), jnp.float32) < slow_share
    base_gap = jnp.where(slow_flag, 0.5 / DEPTH_COUNT, 0.05)
    roughness = jax.random.uniform(generator_seeds[1], (DEPTH_COUNT, SPAN_COUNT_A, 3, SPAN_COUNT_B), jnp.float32, 0.5, 1.5)
    damping_ratio = 1.0 - base_gap[None] * roughness
    pulse_hit_share = jax.random.randint(generator_seeds[2], (DEPTH_COUNT, SPAN_COUNT_A, 1, SPAN_COUNT_B), 0, DEPTH_COUNT) < 2
    pulse_keep_share = jax.random.uniform(generator_seeds[3], (DEPTH_COUNT, SPAN_COUNT_A, 1, SPAN_COUNT_B), jnp.float32, 0.5, 0.8)
    damping_ratio = damping_ratio * jnp.where(pulse_hit_share, pulse_keep_share, 1.0)
    angles = jax.random.uniform(generator_seeds[4], (3, SPAN_COUNT_A, SPAN_COUNT_B), jnp.float32, -math.pi, math.pi)
    rotation = euler_rotation(angles[0], angles[1], angles[2])
    turn_angles = jax.random.uniform(generator_seeds[5], (3, DEPTH_COUNT, SPAN_COUNT_A, SPAN_COUNT_B), jnp.float32, -0.06, 0.06)
    turning = euler_rotation(turn_angles[0], turn_angles[1], turn_angles[2])
    symmetric = []
    for row_index in range(3):
        symmetric_row = []
        for col_index in range(3):
            value = jnp.zeros((DEPTH_COUNT, SPAN_COUNT_A, SPAN_COUNT_B), jnp.float32)
            for inner_index in range(3):
                value = value + rotation[row_index][inner_index][None] * damping_ratio[:, :, inner_index, :] * rotation[col_index][inner_index][None]
            symmetric_row.append(value)
        symmetric.append(symmetric_row)
    entries = []
    for row_index in range(3):
        for col_index in range(3):
            value = jnp.zeros((DEPTH_COUNT, SPAN_COUNT_A, SPAN_COUNT_B), jnp.float32)
            for inner_index in range(3):
                value = value + symmetric[row_index][inner_index] * turning[inner_index][col_index]
            entries.append(value / links)
    return jnp.stack(entries, axis=2)


def plant(result, stream_key, low, largest):
    longest = result.shape.index(max(result.shape))
    spots = []
    for shift in (0, 1):
        where = [jax.random.randint(jax.random.fold_in(stream_key, axis), (), 0, length) for axis, length in enumerate(result.shape)]
        where[longest] = (where[longest] + shift) % result.shape[longest]
        spots.append(tuple(where))
    return result.at[spots[0]].set(low).at[spots[1]].set(largest)


def levels(key, dims, shards, smallest, high):
    def one(position, shards_of):
        heights = jax.random.uniform(jax.random.fold_in(jax.random.fold_in(key, 6), position), (shards_of,), jnp.float32, smallest / len(shards), high / len(shards))
        return jnp.repeat(jnp.exp(heights), dims[position] // shards_of).reshape((-1,) + (1,) * (len(dims) - position - 1))

    factor_of = one(*shards[0])
    for cut in shards[1:]:
        factor_of = factor_of * one(*cut)
    return factor_of


def noise(own_key, shape, scale, limit, cuts=(), kind=jnp.bfloat16):
    result = scale * jax.random.normal(own_key, shape, jnp.float32)
    if cuts:
        result = result * levels(own_key, shape, cuts, -0.22, 0.18)
    return jnp.clip(result, -limit, limit).astype(kind)


def setup_inputs(seed: int = 0) -> dict:
    splits = jax.random.split(jax.random.key(seed), 10)
    mode_shapes = noise(splits[0], (MODES, SPAN_COUNT_A, 3, SPAN_COUNT_B), 1.0, 6.0, ((0, 32),))
    amplitude = noise(splits[1], (MODES,), (0.5 / DEPTH_COUNT), 0.01171875, (), jnp.float32)
    mode_patch = plant(jax.random.randint(splits[2], (MODES,), 0, PATCHES), jax.random.fold_in(splits[2], 1), 0, PATCHES - 1).astype(jnp.int32)
    column_patch = plant(jax.random.randint(splits[3], (SPAN_COUNT_A, SPAN_COUNT_B), 0, PATCHES), jax.random.fold_in(splits[3], 1), 0, PATCHES - 1).astype(jnp.int32)
    wall_mask = plant((jax.random.randint(splits[4], (SPAN_COUNT_A, SPAN_COUNT_B), 0, 4) < 3).astype(jnp.int32), jax.random.fold_in(splits[4], 1), 0, 1)
    offsets = plant(jax.random.randint(splits[5], (SPAN_COUNT_A, SPAN_COUNT_B), 0, 2 * DEPTH_COUNT), jax.random.fold_in(splits[5], 1), 0, (2 * DEPTH_COUNT) - 1).astype(jnp.int32)
    coupling = draw_coupling(jax.random.fold_in(splits[9], 71), 0)
    pivot_inv = draw_pivot_inv(jax.random.fold_in(splits[9], 71), 0)
    stiffness = jnp.clip(jnp.exp(math.log(3.204345557605848e-05) - 0.84729784 * jax.random.uniform(splits[8], (DEPTH_COUNT, SPAN_COUNT_A, SPAN_COUNT_B), jnp.float32) ** levels(splits[8], (DEPTH_COUNT, SPAN_COUNT_A, SPAN_COUNT_B), ((0, 16), (1, 32)), -0.2, 0.2)), 1.373290979245212e-05, 3.204345557605848e-05)
    return dict(mode_shapes=mode_shapes, amplitude=amplitude, mode_patch=mode_patch, column_patch=column_patch, wall_mask=wall_mask, offsets=offsets, coupling=coupling, pivot_inv=pivot_inv, stiffness=stiffness)


def mat_vec(matrix, vector):
    blocks = matrix.reshape(matrix.shape[:-2] + (3, 3, matrix.shape[-1]))
    return jnp.sum(blocks * vector[..., None, :, :], axis=-2)


def forward(pivots, lower_link, right_side, inflow):
    def advance(state_now, layer_data):
        pivot_block, link_row, source_row = layer_data
        updated = mat_vec(pivot_block, source_row + link_row[:, None, :] * state_now)
        return updated, updated

    last_value, forward_values = lax.scan(advance, inflow, (pivots, lower_link, right_side))
    return forward_values, last_value


def backward(pivots, upper_link, forward_values, outflow):
    def advance(state_now, layer_data):
        pivot_block, link_row, value_row = layer_data
        updated = value_row + mat_vec(pivot_block, link_row[:, None, :] * state_now)
        return updated, updated

    first_value, solved = lax.scan(advance, outflow, (pivots, upper_link, forward_values), reverse=True)
    return solved, first_value


def neighbours(displaced):
    zero_column = jnp.zeros_like(displaced[..., :1])
    neighbour_sum = jnp.roll(displaced, 1, axis=1) + jnp.roll(displaced, -1, axis=1)
    neighbour_sum = neighbour_sum + jnp.concatenate([displaced[..., 1:], zero_column], axis=-1)
    return neighbour_sum + jnp.concatenate([zero_column, displaced[..., :-1]], axis=-1)


def reference(mode_shapes, amplitude, mode_patch, column_patch, wall_mask, offsets, coupling, pivot_inv, stiffness):
    select = (mode_patch[:, None, None] == column_patch[None]).astype(jnp.float32)
    weights = amplitude[:, None, None] * select
    wall_shift = jnp.einsum("mij,micj->icj", weights, mode_shapes.astype(jnp.float32))
    wall_shift = wall_shift * wall_mask[:, None, :].astype(jnp.float32)
    depth_index = jnp.arange(DEPTH_COUNT, dtype=jnp.int32)
    lower_link = jnp.where(depth_index[:, None, None] == offsets[None], jnp.zeros_like(coupling), coupling)
    upper_link = jnp.concatenate([lower_link[1:], jnp.zeros_like(lower_link[:1])], axis=0)
    blend_weight = 1.0 - depth_index.astype(jnp.float32) / DEPTH_COUNT
    displaced = blend_weight[:, None, None, None] * wall_shift[None]
    wall_term = lower_link[0][:, None, :] * wall_shift
    zero_state = jnp.zeros((SPAN_COUNT_A, 3, SPAN_COUNT_B), jnp.float32)
    for sweep_index in range(SWEEPS):
        right_side = stiffness[:, :, None, :] * neighbours(displaced)
        right_side = right_side.at[0].add(wall_term)
        forward_values = forward(pivot_inv, lower_link, right_side, zero_state)[0]
        displaced = backward(pivot_inv, upper_link, forward_values, zero_state)[0]
    return displaced
```

```python
import functools
import jax
import jax.numpy as jnp
from jax import lax
from jax.experimental import pallas as pl
from jax.experimental.pallas import tpu as pltpu
from jax.sharding import PartitionSpec as P

SWEEPS = 3
F32 = jnp.float32
LANES = 128
MAP_ROWS = 32
END_ROWS = 8
VMEM_LIMIT = 16 * 1024 * 1024


def call(kernel, outs, scratch, smem, args, name, flops=1000000):
    specs = [
        pl.BlockSpec(memory_space=pltpu.SMEM if i in smem else pltpu.VMEM)
        for i in range(len(args))
    ]
    moved = sum(a.size * a.dtype.itemsize for a in list(args) + list(outs))
    return pl.pallas_call(
        kernel,
        out_shape=outs,
        in_specs=specs,
        out_specs=[pl.BlockSpec(memory_space=pltpu.VMEM) for _ in outs],
        scratch_shapes=scratch,
        name=name,
        cost_estimate=pl.CostEstimate(flops=flops, bytes_accessed=moved, transcendentals=0),
        compiler_params=pltpu.CompilerParams(vmem_limit_bytes=VMEM_LIMIT),
    )(*args)


def shaped(*shape, dtype=F32):
    return jax.ShapeDtypeStruct(shape, dtype)


def wall_parts_kernel(place_ref, amplitude_ref, patch_ref, modes_ref, columns_ref, mask_ref, out_ref):
    own_modes = modes_ref.shape[0]
    parts = out_ref.shape[0]
    base = place_ref[0] * own_modes
    first_mask = mask_ref[0:1, :].astype(F32)
    last_mask = mask_ref[7:8, :].astype(F32)

    def one(pair, carry):
        rows = pl.ds(pl.multiple_of(pair * 16, 16), 16)
        patch = columns_ref[rows, :]
        weights = [
            jnp.where(patch == patch_ref[base + m], amplitude_ref[base + m], 0.0)
            for m in range(own_modes)
        ]
        low, high = pair * 2, pair * 2 + 1
        before = lax.rem(low + parts - 1, parts)
        after = lax.rem(high + 1, parts)
        for c in range(3):
            total = weights[0] * modes_ref[0, c, rows, :].astype(F32)
            for m in range(1, own_modes):
                total = total + weights[m] * modes_ref[m, c, rows, :].astype(F32)
            out_ref[low, 8 * c : 8 * c + 8, :] = total[:8]
            out_ref[high, 8 * c : 8 * c + 8, :] = total[8:]
            out_ref[high, 24 + c : 25 + c, :] = total[7:8]
            out_ref[after, 24 + c : 25 + c, :] = total[15:16]
            out_ref[before, 27 + c : 28 + c, :] = total[0:1]
            out_ref[low, 27 + c : 28 + c, :] = total[8:9]
        out_ref[low, 30:31, :] = first_mask
        out_ref[low, 31:32, :] = last_mask
        out_ref[high, 30:31, :] = first_mask
        out_ref[high, 31:32, :] = last_mask
        return carry

    lax.fori_loop(0, parts // 2, one, 0)


def links_of(place_ref, coupling_ref, offsets_ref):
    cells = coupling_ref.shape[0]
    cut = offsets_ref[...] - place_ref[1] * cells

    def link(k):
        return jnp.where(cut == k, 0.0, coupling_ref[k])

    return link


def product(pivot_ref, k, vector):
    return [
        pivot_ref[k, 3 * a] * vector[0]
        + pivot_ref[k, 3 * a + 1] * vector[1]
        + pivot_ref[k, 3 * a + 2] * vector[2]
        for a in range(3)
    ]


def put_lines(out_ref, row, stride, value):
    for half in range(value.shape[1] // LANES):
        out_ref[pl.ds(half * 8 * stride + row, 8, stride=stride), :] = value[
            :, half * LANES : (half + 1) * LANES
        ]


def get_lines(in_ref, row, stride, width):
    return jnp.concatenate(
        [
            in_ref[pl.ds(half * 8 * stride + row, 8, stride=stride), :]
            for half in range(width // LANES)
        ],
        axis=1,
    )


def maps_kernel(place_ref, pivot_ref, coupling_ref, offsets_ref, out_ref, prefix):
    cells = pivot_ref.shape[0]
    link = links_of(place_ref, coupling_ref, offsets_ref)
    first = link(0)
    for j in range(3):
        column = [pivot_ref[0, 3 * a + j] * first for a in range(3)]
        for a in range(3):
            prefix[0, a] = column[a]
        for k in range(1, cells):
            here = link(k)
            column = product(pivot_ref, k, [here * v for v in column])
            for a in range(3):
                prefix[k, a] = column[a]
        both = column
        upper = [pivot_ref[cells - 1, 3 * a + j] for a in range(3)]
        for a in range(3):
            put_lines(out_ref, 3 * a + j, MAP_ROWS, column[a])
        for k in range(cells - 2, -1, -1):
            above = link(k + 1)
            both = product(pivot_ref, k, [above * v for v in both])
            both = [both[a] + prefix[k, a] for a in range(3)]
            upper = product(pivot_ref, k, [above * v for v in upper])
        for a in range(3):
            put_lines(out_ref, 9 + 3 * a + j, MAP_ROWS, first * upper[a])
            put_lines(out_ref, 18 + 3 * a + j, MAP_ROWS, first * both[a])


def local_ends(pivot_ref, link, right_ref, inflow, values, out_ref):
    cells = pivot_ref.shape[0]
    state = inflow
    for k in range(cells):
        here = link(k)
        state = product(pivot_ref, k, [right_ref[k, b] + here * state[b] for b in range(3)])
        for b in range(3):
            values[k, b] = state[b]
    for b in range(3):
        put_lines(out_ref, b, END_ROWS, state[b])
    for k in range(cells - 2, -1, -1):
        above = link(k + 1)
        lifted = product(pivot_ref, k, [above * v for v in state])
        state = [values[k, b] + lifted[b] for b in range(3)]
    first = link(0)
    for b in range(3):
        put_lines(out_ref, 3 + b, END_ROWS, first * state[b])
    blank = jnp.zeros_like(first)
    put_lines(out_ref, 6, END_ROWS, blank)
    put_lines(out_ref, 7, END_ROWS, blank)


def around(value, low, high):
    rows = lax.broadcasted_iota(jnp.int32, value.shape, 0)
    columns = lax.broadcasted_iota(jnp.int32, value.shape, 1)
    height, width = value.shape
    below = jnp.where(rows == 0, low, pltpu.roll(value, 1, 0))
    above = jnp.where(rows == height - 1, high, pltpu.roll(value, height - 1, 0))
    left = jnp.where(columns == 0, 0.0, pltpu.roll(value, 1, 1))
    right = jnp.where(columns == width - 1, 0.0, pltpu.roll(value, width - 1, 1))
    return (below + above) + (left + right)


def first_kernel(depth, place_ref, parts_ref, mask_ref, pivot_ref, coupling_ref, offsets_ref, stiff_ref,
                 right_ref, wall_ref, out_ref, values, edge_rows):
    cells = pivot_ref.shape[0]
    parts = parts_ref.shape[0]
    total = parts_ref[0]
    for s in range(1, parts):
        total = total + parts_ref[s]
    edge_rows[...] = total[24:32]
    place = place_ref[0]
    low_mask = parts_ref[lax.rem(place + parts - 1, parts), 31:32, :]
    high_mask = parts_ref[lax.rem(place + 1, parts), 30:31, :]
    mask = mask_ref[...].astype(F32)
    start = place_ref[1] == 0
    inflow = []
    for c in range(3):
        shift = total[8 * c : 8 * c + 8] * mask
        summed = around(
            shift, edge_rows[c : c + 1, :] * low_mask, edge_rows[3 + c : 4 + c, :] * high_mask
        )
        held = jnp.where(start, shift, 0.0)
        wall_ref[c] = held
        inflow.append(held)
        for k in range(cells):
            blend = 1.0 - (place_ref[1] * cells + k).astype(F32) * (1.0 / depth)
            right_ref[k, c] = stiff_ref[k] * (blend * summed)
    link = links_of(place_ref, coupling_ref, offsets_ref)
    local_ends(pivot_ref, link, right_ref, inflow, values, out_ref)


def next_kernel(place_ref, shape_ref, low_ref, high_ref, wall_ref, pivot_ref, coupling_ref, offsets_ref,
                stiff_ref, right_ref, out_ref, values, low_rows, high_rows):
    cells = pivot_ref.shape[0]
    low_rows[...] = low_ref[...].astype(F32)
    high_rows[...] = high_ref[...].astype(F32)
    for k in range(cells):
        for c in range(3):
            row = 3 * k + c
            summed = around(
                shape_ref[k, c], low_rows[row : row + 1, :], high_rows[row : row + 1, :]
            )
            right_ref[k, c] = stiff_ref[k] * summed
    link = links_of(place_ref, coupling_ref, offsets_ref)
    local_ends(pivot_ref, link, right_ref, [wall_ref[c] for c in range(3)], values, out_ref)


def chain_kernel(maps_ref, ends_ref, out_ref):
    places = ends_ref.shape[0] // END_ROWS

    def line(ref, row):
        return ref[row : row + 1, :]

    def apply(place, first, vector):
        base = place * MAP_ROWS + first
        return [
            line(maps_ref, base + 3 * a) * vector[0]
            + line(maps_ref, base + 3 * a + 1) * vector[1]
            + line(maps_ref, base + 3 * a + 2) * vector[2]
            for a in range(3)
        ]

    blank = jnp.zeros((1, LANES), F32)
    state = [blank] * 3
    tops = []
    for place in range(places):
        for c in range(3):
            out_ref[place * END_ROWS + c : place * END_ROWS + c + 1, :] = state[c]
        reflected = apply(place, 18, state)
        tops.append([line(ends_ref, place * END_ROWS + 3 + c) + reflected[c] for c in range(3)])
        moved = apply(place, 0, state)
        state = [line(ends_ref, place * END_ROWS + c) + moved[c] for c in range(3)]
    state = [blank] * 3
    for place in range(places - 1, -1, -1):
        base = place * END_ROWS
        for c in range(3):
            out_ref[base + 3 + c : base + 4 + c, :] = state[c]
        out_ref[base + 6 : base + 8, :] = jnp.zeros((2, LANES), F32)
        moved = apply(place, 9, state)
        state = [tops[place][c] + moved[c] for c in range(3)]


def solve_kernel(last, place_ref, flows_ref, wall_ref, right_ref, pivot_ref, coupling_ref, offsets_ref,
                 *rest):
    cells = pivot_ref.shape[0]
    width = wall_ref.shape[2]
    if last:
        shape_ref, values = rest
    else:
        shape_ref, first_ref, last_ref, values, first_rows, last_rows = rest
    link = links_of(place_ref, coupling_ref, offsets_ref)
    state = [wall_ref[c] + get_lines(flows_ref, c, END_ROWS, width) for c in range(3)]
    for k in range(cells):
        here = link(k)
        state = product(pivot_ref, k, [right_ref[k, b] + here * state[b] for b in range(3)])
        for b in range(3):
            values[k, b] = state[b]
    lifted = [get_lines(flows_ref, 3 + c, END_ROWS, width) for c in range(3)]
    for k in range(cells - 1, -1, -1):
        lifted = product(pivot_ref, k, lifted)
        state = [values[k, b] + lifted[b] for b in range(3)]
        for b in range(3):
            shape_ref[k, b] = state[b]
            if not last:
                row = 3 * k + b
                first_rows[row : row + 1, :] = state[b][0:1]
                last_rows[row : row + 1, :] = state[b][7:8]
        if k:
            here = link(k)
            lifted = [here * v for v in state]
    if not last:
        first_ref[...] = first_rows[...].astype(jnp.bfloat16)
        last_ref[...] = last_rows[...].astype(jnp.bfloat16)


def per_device(
    mode_shapes,
    amplitude,
    mode_patch,
    column_patch,
    wall_mask,
    offsets,
    coupling,
    pivot_inv,
    stiffness,
):
    rows, width = wall_mask.shape
    cells = coupling.shape[0]
    surf, norm = lax.axis_size("surf"), lax.axis_size("norm")
    place = jnp.stack([lax.axis_index("surf"), lax.axis_index("norm")]).astype(jnp.int32)
    modes = jnp.transpose(mode_shapes, (0, 2, 1, 3))
    pivots = jnp.transpose(pivot_inv, (0, 2, 1, 3))
    cube = shaped(cells, 3, rows, width)
    scratch = pltpu.VMEM((cells, 3, rows, width), F32)
    edge = shaped(cells * 3, width, dtype=jnp.bfloat16)
    edge_scratch = pltpu.VMEM((cells * 3, width), F32)
    ends_shape = shaped(norm * END_ROWS, LANES)

    def swapped(block, axis, count):
        block = block.reshape((count, block.shape[0] // count) + block.shape[1:])
        block = lax.all_to_all(block, axis, 0, 0, tiled=True)
        return block.reshape((-1,) + block.shape[2:])

    (parts,) = call(
        wall_parts_kernel,
        [shaped(surf, 32, width)],
        [],
        (0, 1, 2),
        (place, amplitude, mode_patch, modes, column_patch, wall_mask),
        "wall_parts",
    )
    parts = lax.all_to_all(parts, "surf", 0, 0, tiled=True)
    (maps,) = call(
        maps_kernel,
        [shaped(norm * MAP_ROWS, LANES)],
        [scratch],
        (0,),
        (place, pivots, coupling, offsets),
        "maps",
        flops=10000000,
    )
    maps = swapped(maps, "norm", norm)
    right, wall, ends = call(
        functools.partial(first_kernel, cells * norm),
        [cube, shaped(3, rows, width), ends_shape],
        [scratch, pltpu.VMEM((8, width), F32)],
        (0,),
        (place, parts, wall_mask, pivots, coupling, offsets, stiffness),
        "first_ends",
    )
    for sweep in range(SWEEPS):
        ends = swapped(ends, "norm", norm)
        (flows,) = call(chain_kernel, [ends_shape], [], (), (maps, ends), "chain")
        flows = swapped(flows, "norm", norm)
        last = sweep == SWEEPS - 1
        solved = call(
            functools.partial(solve_kernel, last),
            [cube] if last else [cube, edge, edge],
            [scratch] if last else [scratch, edge_scratch, edge_scratch],
            (0,),
            (place, flows, wall, right, pivots, coupling, offsets),
            "solve",
        )
        if last:
            return jnp.transpose(solved[0], (0, 2, 1, 3))
        shape, first_edge, last_edge = solved
        low = lax.ppermute(last_edge, "surf", [(i, (i + 1) % surf) for i in range(surf)])
        high = lax.ppermute(first_edge, "surf", [(i, (i - 1) % surf) for i in range(surf)])
        right, ends = call(
            next_kernel,
            [cube, ends_shape],
            [scratch, edge_scratch, edge_scratch],
            (0,),
            (place, shape, low, high, wall, pivots, coupling, offsets, stiffness),
            "next_ends",
        )


def solution(mesh):
    return jax.shard_map(
        per_device,
        mesh=mesh,
        in_specs=(
            P("surf", None, None, None),
            P(),
            P(),
            P(),
            P("surf", None),
            P("surf", None),
            P("norm", "surf", None),
            P("norm", "surf", None, None),
            P("norm", "surf", None),
        ),
        out_specs=P("norm", "surf", None, None),
        check_vma=False,
    )
```

```python
import functools
import jax
import jax.numpy as jnp
from jax import lax
from jax.experimental import pallas as pl
from jax.experimental.pallas import tpu as pltpu
from jax.sharding import PartitionSpec as P

SWEEPS = 3
F32 = jnp.float32
LANES = 128
MAP_ROWS = 40
MAP_ENDS = 27
END_ROWS = 8
VMEM_LIMIT = 16 * 1024 * 1024


def call(kernel, outs, scratch, smem, args, name, flops=1000000):
    specs = [
        pl.BlockSpec(memory_space=pltpu.SMEM if i in smem else pltpu.VMEM)
        for i in range(len(args))
    ]
    moved = sum(a.size * a.dtype.itemsize for a in list(args) + list(outs))
    return pl.pallas_call(
        kernel,
        out_shape=outs,
        in_specs=specs,
        out_specs=[pl.BlockSpec(memory_space=pltpu.VMEM) for _ in outs],
        scratch_shapes=scratch,
        name=name,
        cost_estimate=pl.CostEstimate(flops=flops, bytes_accessed=moved, transcendentals=0),
        compiler_params=pltpu.CompilerParams(vmem_limit_bytes=VMEM_LIMIT),
    )(*args)


def shaped(*shape, dtype=F32):
    return jax.ShapeDtypeStruct(shape, dtype)


def wall_parts_kernel(place_ref, amplitude_ref, patch_ref, modes_ref, columns_ref, mask_ref, out_ref):
    own_modes = modes_ref.shape[0]
    parts = out_ref.shape[0]
    base = place_ref[0] * own_modes
    first_mask = mask_ref[0:1, :].astype(F32)
    last_mask = mask_ref[7:8, :].astype(F32)

    def one(pair, carry):
        rows = pl.ds(pl.multiple_of(pair * 16, 16), 16)
        patch = columns_ref[rows, :]
        weights = [
            jnp.where(patch == patch_ref[base + m], amplitude_ref[base + m], 0.0)
            for m in range(own_modes)
        ]
        low, high = pair * 2, pair * 2 + 1
        before = lax.rem(low + parts - 1, parts)
        after = lax.rem(high + 1, parts)
        for c in range(3):
            total = weights[0] * modes_ref[0, c, rows, :].astype(F32)
            for m in range(1, own_modes):
                total = total + weights[m] * modes_ref[m, c, rows, :].astype(F32)
            out_ref[low, 8 * c : 8 * c + 8, :] = total[:8]
            out_ref[high, 8 * c : 8 * c + 8, :] = total[8:]
            out_ref[high, 24 + c : 25 + c, :] = total[7:8]
            out_ref[after, 24 + c : 25 + c, :] = total[15:16]
            out_ref[before, 27 + c : 28 + c, :] = total[0:1]
            out_ref[low, 27 + c : 28 + c, :] = total[8:9]
        out_ref[low, 30:31, :] = first_mask
        out_ref[low, 31:32, :] = last_mask
        out_ref[high, 30:31, :] = first_mask
        out_ref[high, 31:32, :] = last_mask
        return carry

    lax.fori_loop(0, parts // 2, one, 0)


def links_of(place_ref, coupling_ref, offsets_ref):
    cells = coupling_ref.shape[0]
    cut = offsets_ref[...] - place_ref[1] * cells

    def link(k):
        return jnp.where(cut == k, 0.0, coupling_ref[k])

    return link


def product(pivot_ref, k, vector):
    return [
        pivot_ref[k, 3 * a] * vector[0]
        + pivot_ref[k, 3 * a + 1] * vector[1]
        + pivot_ref[k, 3 * a + 2] * vector[2]
        for a in range(3)
    ]


def put_lines(out_ref, row, stride, value):
    for half in range(value.shape[1] // LANES):
        out_ref[pl.ds(half * 8 * stride + row, 8, stride=stride), :] = value[
            :, half * LANES : (half + 1) * LANES
        ]


def get_lines(in_ref, row, stride, width):
    return jnp.concatenate(
        [
            in_ref[pl.ds(half * 8 * stride + row, 8, stride=stride), :]
            for half in range(width // LANES)
        ],
        axis=1,
    )


def maps_kernel(place_ref, pivot_ref, coupling_ref, offsets_ref, out_ref, prefix):
    cells = pivot_ref.shape[0]
    link = links_of(place_ref, coupling_ref, offsets_ref)
    first = link(0)
    for j in range(3):
        column = [pivot_ref[0, 3 * a + j] * first for a in range(3)]
        for a in range(3):
            prefix[0, a] = column[a]
        for k in range(1, cells):
            here = link(k)
            column = product(pivot_ref, k, [here * v for v in column])
            for a in range(3):
                prefix[k, a] = column[a]
        both = column
        upper = [pivot_ref[cells - 1, 3 * a + j] for a in range(3)]
        for a in range(3):
            put_lines(out_ref, 3 * a + j, MAP_ROWS, column[a])
        for k in range(cells - 2, -1, -1):
            above = link(k + 1)
            both = product(pivot_ref, k, [above * v for v in both])
            both = [both[a] + prefix[k, a] for a in range(3)]
            upper = product(pivot_ref, k, [above * v for v in upper])
        for a in range(3):
            put_lines(out_ref, 9 + 3 * a + j, MAP_ROWS, first * upper[a])
            put_lines(out_ref, 18 + 3 * a + j, MAP_ROWS, first * both[a])


def local_ends(pivot_ref, link, right_ref, inflow, values, out_ref, row=0, stride=END_ROWS):
    cells = pivot_ref.shape[0]
    state = inflow
    for k in range(cells):
        here = link(k)
        state = product(pivot_ref, k, [right_ref[k, b] + here * state[b] for b in range(3)])
        for b in range(3):
            values[k, b] = state[b]
    for b in range(3):
        put_lines(out_ref, row + b, stride, state[b])
    for k in range(cells - 2, -1, -1):
        above = link(k + 1)
        lifted = product(pivot_ref, k, [above * v for v in state])
        state = [values[k, b] + lifted[b] for b in range(3)]
    first = link(0)
    for b in range(3):
        put_lines(out_ref, row + 3 + b, stride, first * state[b])
    blank = jnp.zeros_like(first)
    for b in range(row + 6, stride):
        put_lines(out_ref, b, stride, blank)


def around(value, low, high):
    rows = lax.broadcasted_iota(jnp.int32, value.shape, 0)
    columns = lax.broadcasted_iota(jnp.int32, value.shape, 1)
    height, width = value.shape
    below = jnp.where(rows == 0, low, pltpu.roll(value, 1, 0))
    above = jnp.where(rows == height - 1, high, pltpu.roll(value, height - 1, 0))
    left = jnp.where(columns == 0, 0.0, pltpu.roll(value, 1, 1))
    right = jnp.where(columns == width - 1, 0.0, pltpu.roll(value, width - 1, 1))
    return (below + above) + (left + right)


def first_kernel(depth, place_ref, parts_ref, maps_ref, mask_ref, pivot_ref, coupling_ref, offsets_ref,
                 stiff_ref, right_ref, wall_ref, out_ref, values, edge_rows):
    cells = pivot_ref.shape[0]
    parts = parts_ref.shape[0]
    total = parts_ref[0]
    for s in range(1, parts):
        total = total + parts_ref[s]
    edge_rows[...] = total[24:32]
    place = place_ref[0]
    low_mask = parts_ref[lax.rem(place + parts - 1, parts), 31:32, :]
    high_mask = parts_ref[lax.rem(place + 1, parts), 30:31, :]
    mask = mask_ref[...].astype(F32)
    start = place_ref[1] == 0
    inflow = []
    for c in range(3):
        shift = total[8 * c : 8 * c + 8] * mask
        summed = around(
            shift, edge_rows[c : c + 1, :] * low_mask, edge_rows[3 + c : 4 + c, :] * high_mask
        )
        held = jnp.where(start, shift, 0.0)
        wall_ref[c] = held
        inflow.append(held)
        for k in range(cells):
            blend = 1.0 - (place_ref[1] * cells + k).astype(F32) * (1.0 / depth)
            right_ref[k, c] = stiff_ref[k] * (blend * summed)
    link = links_of(place_ref, coupling_ref, offsets_ref)
    out_ref[...] = maps_ref[...]
    local_ends(pivot_ref, link, right_ref, inflow, values, out_ref, MAP_ENDS, MAP_ROWS)


def next_kernel(place_ref, shape_ref, low_ref, high_ref, wall_ref, pivot_ref, coupling_ref, offsets_ref,
                stiff_ref, right_ref, out_ref, values, low_rows, high_rows):
    cells = pivot_ref.shape[0]
    low_rows[...] = low_ref[...].astype(F32)
    high_rows[...] = high_ref[...].astype(F32)
    for k in range(cells):
        for c in range(3):
            row = 3 * k + c
            summed = around(
                shape_ref[k, c], low_rows[row : row + 1, :], high_rows[row : row + 1, :]
            )
            right_ref[k, c] = stiff_ref[k] * summed
    link = links_of(place_ref, coupling_ref, offsets_ref)
    local_ends(pivot_ref, link, right_ref, [wall_ref[c] for c in range(3)], values, out_ref)


def chain_kernel(maps_ref, *rest):
    out_ref = rest[-1]
    ends_ref, offset, stride = (rest[0], 0, END_ROWS) if len(rest) == 2 else (maps_ref, MAP_ENDS, MAP_ROWS)
    places = out_ref.shape[0] // END_ROWS

    def line(ref, row):
        return ref[row : row + 1, :]

    def apply(place, first, vector):
        base = place * MAP_ROWS + first
        return [
            line(maps_ref, base + 3 * a) * vector[0]
            + line(maps_ref, base + 3 * a + 1) * vector[1]
            + line(maps_ref, base + 3 * a + 2) * vector[2]
            for a in range(3)
        ]

    blank = jnp.zeros((1, LANES), F32)
    state = [blank] * 3
    tops = []
    for place in range(places):
        for c in range(3):
            out_ref[place * END_ROWS + c : place * END_ROWS + c + 1, :] = state[c]
        reflected = apply(place, 18, state)
        tops.append([line(ends_ref, place * stride + offset + 3 + c) + reflected[c] for c in range(3)])
        moved = apply(place, 0, state)
        state = [line(ends_ref, place * stride + offset + c) + moved[c] for c in range(3)]
    state = [blank] * 3
    for place in range(places - 1, -1, -1):
        base = place * END_ROWS
        for c in range(3):
            out_ref[base + 3 + c : base + 4 + c, :] = state[c]
        out_ref[base + 6 : base + 8, :] = jnp.zeros((2, LANES), F32)
        moved = apply(place, 9, state)
        state = [tops[place][c] + moved[c] for c in range(3)]


def solve_kernel(last, place_ref, flows_ref, wall_ref, right_ref, pivot_ref, coupling_ref, offsets_ref,
                 *rest):
    cells = pivot_ref.shape[0]
    width = wall_ref.shape[2]
    if last:
        shape_ref, values = rest
    else:
        shape_ref, first_ref, last_ref, values, first_rows, last_rows = rest
    link = links_of(place_ref, coupling_ref, offsets_ref)
    state = [wall_ref[c] + get_lines(flows_ref, c, END_ROWS, width) for c in range(3)]
    for k in range(cells):
        here = link(k)
        state = product(pivot_ref, k, [right_ref[k, b] + here * state[b] for b in range(3)])
        for b in range(3):
            values[k, b] = state[b]
    lifted = [get_lines(flows_ref, 3 + c, END_ROWS, width) for c in range(3)]
    for k in range(cells - 1, -1, -1):
        lifted = product(pivot_ref, k, lifted)
        state = [values[k, b] + lifted[b] for b in range(3)]
        for b in range(3):
            shape_ref[k, b] = state[b]
            if not last:
                row = 3 * k + b
                first_rows[row : row + 1, :] = state[b][0:1]
                last_rows[row : row + 1, :] = state[b][7:8]
        if k:
            here = link(k)
            lifted = [here * v for v in state]
    if not last:
        first_ref[...] = first_rows[...].astype(jnp.bfloat16)
        last_ref[...] = last_rows[...].astype(jnp.bfloat16)


def per_device(
    mode_shapes,
    amplitude,
    mode_patch,
    column_patch,
    wall_mask,
    offsets,
    coupling,
    pivot_inv,
    stiffness,
):
    rows, width = wall_mask.shape
    cells = coupling.shape[0]
    surf, norm = lax.axis_size("surf"), lax.axis_size("norm")
    place = jnp.stack([lax.axis_index("surf"), lax.axis_index("norm")]).astype(jnp.int32)
    modes = jnp.transpose(mode_shapes, (0, 2, 1, 3))
    pivots = jnp.transpose(pivot_inv, (0, 2, 1, 3))
    cube = shaped(cells, 3, rows, width)
    scratch = pltpu.VMEM((cells, 3, rows, width), F32)
    edge = shaped(cells * 3, width, dtype=jnp.bfloat16)
    edge_scratch = pltpu.VMEM((cells * 3, width), F32)
    ends_shape = shaped(norm * END_ROWS, LANES)

    def swapped(block, axis, count):
        block = block.reshape((count, block.shape[0] // count) + block.shape[1:])
        block = lax.all_to_all(block, axis, 0, 0, tiled=True)
        return block.reshape((-1,) + block.shape[2:])

    (parts,) = call(
        wall_parts_kernel,
        [shaped(surf, 32, width)],
        [],
        (0, 1, 2),
        (place, amplitude, mode_patch, modes, column_patch, wall_mask),
        "wall_parts",
    )
    parts = lax.all_to_all(parts, "surf", 0, 0, tiled=True)
    (maps,) = call(
        maps_kernel,
        [shaped(norm * MAP_ROWS, LANES)],
        [scratch],
        (0,),
        (place, pivots, coupling, offsets),
        "maps",
        flops=10000000,
    )
    right, wall, ends = call(
        functools.partial(first_kernel, cells * norm),
        [cube, shaped(3, rows, width), shaped(norm * MAP_ROWS, LANES)],
        [scratch, pltpu.VMEM((8, width), F32)],
        (0,),
        (place, parts, maps, wall_mask, pivots, coupling, offsets, stiffness),
        "first_ends",
    )
    for sweep in range(SWEEPS):
        ends = swapped(ends, "norm", norm)
        if sweep == 0:
            maps = ends
        given = (maps,) if sweep == 0 else (maps, ends)
        (flows,) = call(chain_kernel, [ends_shape], [], (), given, "chain")
        flows = swapped(flows, "norm", norm)
        last = sweep == SWEEPS - 1
        solved = call(
            functools.partial(solve_kernel, last),
            [cube] if last else [cube, edge, edge],
            [scratch] if last else [scratch, edge_scratch, edge_scratch],
            (0,),
            (place, flows, wall, right, pivots, coupling, offsets),
            "solve",
        )
        if last:
            return jnp.transpose(solved[0], (0, 2, 1, 3))
        shape, first_edge, last_edge = solved
        low = lax.ppermute(last_edge, "surf", [(i, (i + 1) % surf) for i in range(surf)])
        high = lax.ppermute(first_edge, "surf", [(i, (i - 1) % surf) for i in range(surf)])
        right, ends = call(
            next_kernel,
            [cube, ends_shape],
            [scratch, edge_scratch, edge_scratch],
            (0,),
            (place, shape, low, high, wall, pivots, coupling, offsets, stiffness),
            "next_ends",
        )


def solution(mesh):
    return jax.shard_map(
        per_device,
        mesh=mesh,
        in_specs=(
            P("surf", None, None, None),
            P(),
            P(),
            P(),
            P("surf", None),
            P("surf", None),
            P("norm", "surf", None),
            P("norm", "surf", None, None),
            P("norm", "surf", None),
        ),
        out_specs=P("norm", "surf", None, None),
        check_vma=False,
    )
```

```python
import functools
import jax
import jax.numpy as jnp
from jax import lax
from jax.experimental import pallas as pl
from jax.experimental.pallas import tpu as pltpu
from jax.sharding import PartitionSpec as P

SWEEPS = 3
F32 = jnp.float32
LANES = 128
MAP_ROWS = 40
MAP_ENDS = 27
END_ROWS = 8
VMEM_LIMIT = 16 * 1024 * 1024


def call(kernel, outs, scratch, smem, args, name, flops=1000000):
    specs = [
        pl.BlockSpec(memory_space=pltpu.SMEM if i in smem else pltpu.VMEM)
        for i in range(len(args))
    ]
    moved = sum(a.size * a.dtype.itemsize for a in list(args) + list(outs))
    return pl.pallas_call(
        kernel,
        out_shape=outs,
        in_specs=specs,
        out_specs=[pl.BlockSpec(memory_space=pltpu.VMEM) for _ in outs],
        scratch_shapes=scratch,
        name=name,
        cost_estimate=pl.CostEstimate(flops=flops, bytes_accessed=moved, transcendentals=0),
        compiler_params=pltpu.CompilerParams(vmem_limit_bytes=VMEM_LIMIT),
    )(*args)


def shaped(*shape, dtype=F32):
    return jax.ShapeDtypeStruct(shape, dtype)


def wall_parts_kernel(place_ref, amplitude_ref, patch_ref, modes_ref, columns_ref, mask_ref, out_ref):
    own_modes = modes_ref.shape[0]
    parts = out_ref.shape[0]
    base = place_ref[0] * own_modes
    first_mask = mask_ref[0:1, :].astype(F32)
    last_mask = mask_ref[7:8, :].astype(F32)

    def one(pair, carry):
        rows = pl.ds(pl.multiple_of(pair * 16, 16), 16)
        patch = columns_ref[rows, :]
        weights = [
            jnp.where(patch == patch_ref[base + m], amplitude_ref[base + m], 0.0)
            for m in range(own_modes)
        ]
        low, high = pair * 2, pair * 2 + 1
        before = lax.rem(low + parts - 1, parts)
        after = lax.rem(high + 1, parts)
        for c in range(3):
            total = weights[0] * modes_ref[0, c, rows, :].astype(F32)
            for m in range(1, own_modes):
                total = total + weights[m] * modes_ref[m, c, rows, :].astype(F32)
            out_ref[low, 8 * c : 8 * c + 8, :] = total[:8]
            out_ref[high, 8 * c : 8 * c + 8, :] = total[8:]
            out_ref[high, 24 + c : 25 + c, :] = total[7:8]
            out_ref[after, 24 + c : 25 + c, :] = total[15:16]
            out_ref[before, 27 + c : 28 + c, :] = total[0:1]
            out_ref[low, 27 + c : 28 + c, :] = total[8:9]
        out_ref[low, 30:31, :] = first_mask
        out_ref[low, 31:32, :] = last_mask
        out_ref[high, 30:31, :] = first_mask
        out_ref[high, 31:32, :] = last_mask
        return carry

    lax.fori_loop(0, parts // 2, one, 0)


def links_of(place_ref, coupling_ref, offsets_ref):
    cells = coupling_ref.shape[0]
    cut = offsets_ref[...] - place_ref[1] * cells

    def link(k):
        return jnp.where(cut == k, 0.0, coupling_ref[k])

    return link


def product(pivot_ref, k, vector):
    return [
        pivot_ref[k, 3 * a] * vector[0]
        + pivot_ref[k, 3 * a + 1] * vector[1]
        + pivot_ref[k, 3 * a + 2] * vector[2]
        for a in range(3)
    ]


def put_lines(out_ref, row, stride, value):
    for half in range(value.shape[1] // LANES):
        out_ref[pl.ds(half * 8 * stride + row, 8, stride=stride), :] = value[
            :, half * LANES : (half + 1) * LANES
        ]


def get_lines(in_ref, row, stride, width):
    return jnp.concatenate(
        [
            in_ref[pl.ds(half * 8 * stride + row, 8, stride=stride), :]
            for half in range(width // LANES)
        ],
        axis=1,
    )


def maps_kernel(place_ref, pivot_ref, coupling_ref, offsets_ref, out_ref, prefix):
    cells = pivot_ref.shape[0]
    link = links_of(place_ref, coupling_ref, offsets_ref)
    first = link(0)
    for j in range(3):
        column = [pivot_ref[0, 3 * a + j] * first for a in range(3)]
        for a in range(3):
            prefix[0, a] = column[a]
        for k in range(1, cells):
            here = link(k)
            column = product(pivot_ref, k, [here * v for v in column])
            for a in range(3):
                prefix[k, a] = column[a]
        both = column
        upper = [pivot_ref[cells - 1, 3 * a + j] for a in range(3)]
        for a in range(3):
            put_lines(out_ref, 3 * a + j, MAP_ROWS, column[a])
        for k in range(cells - 2, -1, -1):
            above = link(k + 1)
            both = product(pivot_ref, k, [above * v for v in both])
            both = [both[a] + prefix[k, a] for a in range(3)]
            upper = product(pivot_ref, k, [above * v for v in upper])
        for a in range(3):
            put_lines(out_ref, 9 + 3 * a + j, MAP_ROWS, first * upper[a])
            put_lines(out_ref, 18 + 3 * a + j, MAP_ROWS, first * both[a])


def local_ends(pivot_ref, link, right_ref, inflow, values, out_ref, row=0, stride=END_ROWS):
    cells = pivot_ref.shape[0]
    state = inflow
    for k in range(cells):
        here = link(k)
        state = product(pivot_ref, k, [right_ref[k, b] + here * state[b] for b in range(3)])
        for b in range(3):
            values[k, b] = state[b]
    for b in range(3):
        put_lines(out_ref, row + b, stride, state[b])
    for k in range(cells - 2, -1, -1):
        above = link(k + 1)
        lifted = product(pivot_ref, k, [above * v for v in state])
        state = [values[k, b] + lifted[b] for b in range(3)]
    first = link(0)
    for b in range(3):
        put_lines(out_ref, row + 3 + b, stride, first * state[b])
    blank = jnp.zeros_like(first)
    for b in range(row + 6, stride):
        put_lines(out_ref, b, stride, blank)


def around(value, low, high):
    rows = lax.broadcasted_iota(jnp.int32, value.shape, 0)
    columns = lax.broadcasted_iota(jnp.int32, value.shape, 1)
    height, width = value.shape
    below = jnp.where(rows == 0, low, pltpu.roll(value, 1, 0))
    above = jnp.where(rows == height - 1, high, pltpu.roll(value, height - 1, 0))
    left = jnp.where(columns == 0, 0.0, pltpu.roll(value, 1, 1))
    right = jnp.where(columns == width - 1, 0.0, pltpu.roll(value, width - 1, 1))
    return (below + above) + (left + right)


def first_kernel(depth, place_ref, parts_ref, maps_ref, mask_ref, pivot_ref, coupling_ref, offsets_ref,
                 stiff_ref, right_ref, wall_ref, out_ref, values, edge_rows):
    cells = pivot_ref.shape[0]
    parts = parts_ref.shape[0]
    total = parts_ref[0]
    for s in range(1, parts):
        total = total + parts_ref[s]
    edge_rows[...] = total[24:32]
    place = place_ref[0]
    low_mask = parts_ref[lax.rem(place + parts - 1, parts), 31:32, :]
    high_mask = parts_ref[lax.rem(place + 1, parts), 30:31, :]
    mask = mask_ref[...].astype(F32)
    start = place_ref[1] == 0
    inflow = []
    for c in range(3):
        shift = total[8 * c : 8 * c + 8] * mask
        summed = around(
            shift, edge_rows[c : c + 1, :] * low_mask, edge_rows[3 + c : 4 + c, :] * high_mask
        )
        held = jnp.where(start, shift, 0.0)
        wall_ref[c] = held
        inflow.append(held)
        for k in range(cells):
            blend = 1.0 - (place_ref[1] * cells + k).astype(F32) * (1.0 / depth)
            right_ref[k, c] = stiff_ref[k] * (blend * summed)
    link = links_of(place_ref, coupling_ref, offsets_ref)
    out_ref[...] = maps_ref[...]
    local_ends(pivot_ref, link, right_ref, inflow, values, out_ref, MAP_ENDS, MAP_ROWS)


def next_kernel(place_ref, shape_ref, inner_ref, outer_ref, wall_ref, pivot_ref, coupling_ref, offsets_ref,
                stiff_ref, right_ref, out_ref, values, low_rows, high_rows):
    cells = pivot_ref.shape[0]
    even = lax.rem(place_ref[0], 2) == 0
    inner, outer = inner_ref[...].astype(F32), outer_ref[...].astype(F32)
    low_rows[...] = jnp.where(even, outer, inner)
    high_rows[...] = jnp.where(even, inner, outer)
    for k in range(cells):
        for c in range(3):
            row = 3 * k + c
            summed = around(
                shape_ref[k, c], low_rows[row : row + 1, :], high_rows[row : row + 1, :]
            )
            right_ref[k, c] = stiff_ref[k] * summed
    link = links_of(place_ref, coupling_ref, offsets_ref)
    local_ends(pivot_ref, link, right_ref, [wall_ref[c] for c in range(3)], values, out_ref)


def chain_kernel(maps_ref, *rest):
    out_ref = rest[-1]
    ends_ref, offset, stride = (rest[0], 0, END_ROWS) if len(rest) == 2 else (maps_ref, MAP_ENDS, MAP_ROWS)
    places = out_ref.shape[0] // END_ROWS

    def line(ref, row):
        return ref[row : row + 1, :]

    def apply(place, first, vector):
        base = place * MAP_ROWS + first
        return [
            line(maps_ref, base + 3 * a) * vector[0]
            + line(maps_ref, base + 3 * a + 1) * vector[1]
            + line(maps_ref, base + 3 * a + 2) * vector[2]
            for a in range(3)
        ]

    blank = jnp.zeros((1, LANES), F32)
    state = [blank] * 3
    tops = []
    for place in range(places):
        for c in range(3):
            out_ref[place * END_ROWS + c : place * END_ROWS + c + 1, :] = state[c]
        reflected = apply(place, 18, state)
        tops.append([line(ends_ref, place * stride + offset + 3 + c) + reflected[c] for c in range(3)])
        moved = apply(place, 0, state)
        state = [line(ends_ref, place * stride + offset + c) + moved[c] for c in range(3)]
    state = [blank] * 3
    for place in range(places - 1, -1, -1):
        base = place * END_ROWS
        for c in range(3):
            out_ref[base + 3 + c : base + 4 + c, :] = state[c]
        out_ref[base + 6 : base + 8, :] = jnp.zeros((2, LANES), F32)
        moved = apply(place, 9, state)
        state = [tops[place][c] + moved[c] for c in range(3)]


def solve_kernel(last, place_ref, flows_ref, wall_ref, right_ref, pivot_ref, coupling_ref, offsets_ref,
                 *rest):
    cells = pivot_ref.shape[0]
    width = wall_ref.shape[2]
    if last:
        shape_ref, values = rest
    else:
        shape_ref, inner_ref, outer_ref, values, first_rows, last_rows = rest
    link = links_of(place_ref, coupling_ref, offsets_ref)
    state = [wall_ref[c] + get_lines(flows_ref, c, END_ROWS, width) for c in range(3)]
    for k in range(cells):
        here = link(k)
        state = product(pivot_ref, k, [right_ref[k, b] + here * state[b] for b in range(3)])
        for b in range(3):
            values[k, b] = state[b]
    lifted = [get_lines(flows_ref, 3 + c, END_ROWS, width) for c in range(3)]
    for k in range(cells - 1, -1, -1):
        lifted = product(pivot_ref, k, lifted)
        state = [values[k, b] + lifted[b] for b in range(3)]
        for b in range(3):
            shape_ref[k, b] = state[b]
            if not last:
                row = 3 * k + b
                first_rows[row : row + 1, :] = state[b][0:1]
                last_rows[row : row + 1, :] = state[b][7:8]
        if k:
            here = link(k)
            lifted = [here * v for v in state]
    if not last:
        even = lax.rem(place_ref[0], 2) == 0
        first, final = first_rows[...], last_rows[...]
        inner_ref[...] = jnp.where(even, final, first).astype(jnp.bfloat16)
        outer_ref[...] = jnp.where(even, first, final).astype(jnp.bfloat16)


def per_device(
    mode_shapes,
    amplitude,
    mode_patch,
    column_patch,
    wall_mask,
    offsets,
    coupling,
    pivot_inv,
    stiffness,
):
    rows, width = wall_mask.shape
    cells = coupling.shape[0]
    surf, norm = lax.axis_size("surf"), lax.axis_size("norm")
    place = jnp.stack([lax.axis_index("surf"), lax.axis_index("norm")]).astype(jnp.int32)
    modes = jnp.transpose(mode_shapes, (0, 2, 1, 3))
    pivots = jnp.transpose(pivot_inv, (0, 2, 1, 3))
    cube = shaped(cells, 3, rows, width)
    scratch = pltpu.VMEM((cells, 3, rows, width), F32)
    edge = shaped(cells * 3, width, dtype=jnp.bfloat16)
    edge_scratch = pltpu.VMEM((cells * 3, width), F32)
    ends_shape = shaped(norm * END_ROWS, LANES)

    def swapped(block, axis, count):
        block = block.reshape((count, block.shape[0] // count) + block.shape[1:])
        block = lax.all_to_all(block, axis, 0, 0, tiled=True)
        return block.reshape((-1,) + block.shape[2:])

    (parts,) = call(
        wall_parts_kernel,
        [shaped(surf, 32, width)],
        [],
        (0, 1, 2),
        (place, amplitude, mode_patch, modes, column_patch, wall_mask),
        "wall_parts",
    )
    parts = lax.all_to_all(parts, "surf", 0, 0, tiled=True)
    (maps,) = call(
        maps_kernel,
        [shaped(norm * MAP_ROWS, LANES)],
        [scratch],
        (0,),
        (place, pivots, coupling, offsets),
        "maps",
        flops=10000000,
    )
    right, wall, ends = call(
        functools.partial(first_kernel, cells * norm),
        [cube, shaped(3, rows, width), shaped(norm * MAP_ROWS, LANES)],
        [scratch, pltpu.VMEM((8, width), F32)],
        (0,),
        (place, parts, maps, wall_mask, pivots, coupling, offsets, stiffness),
        "first_ends",
    )
    for sweep in range(SWEEPS):
        ends = swapped(ends, "norm", norm)
        if sweep == 0:
            maps = ends
        given = (maps,) if sweep == 0 else (maps, ends)
        (flows,) = call(chain_kernel, [ends_shape], [], (), given, "chain")
        flows = swapped(flows, "norm", norm)
        last = sweep == SWEEPS - 1
        solved = call(
            functools.partial(solve_kernel, last),
            [cube] if last else [cube, edge, edge],
            [scratch] if last else [scratch, edge_scratch, edge_scratch],
            (0,),
            (place, flows, wall, right, pivots, coupling, offsets),
            "solve",
        )
        if last:
            return jnp.transpose(solved[0], (0, 2, 1, 3))
        shape, inner, outer = solved
        inner = lax.ppermute(inner, "surf", [(i, i + 1 - 2 * (i % 2)) for i in range(surf)])
        outer = lax.ppermute(
            outer, "surf", [(i, (i - 1 + 2 * (i % 2)) % surf) for i in range(surf)]
        )
        right, ends = call(
            next_kernel,
            [cube, ends_shape],
            [scratch, edge_scratch, edge_scratch],
            (0,),
            (place, shape, inner, outer, wall, pivots, coupling, offsets, stiffness),
            "next_ends",
        )


def solution(mesh):
    return jax.shard_map(
        per_device,
        mesh=mesh,
        in_specs=(
            P("surf", None, None, None),
            P(),
            P(),
            P(),
            P("surf", None),
            P("surf", None),
            P("norm", "surf", None),
            P("norm", "surf", None, None),
            P("norm", "surf", None),
        ),
        out_specs=P("norm", "surf", None, None),
        check_vma=False,
    )
```

```python
import functools
import jax
import jax.numpy as jnp
from jax import lax
from jax.experimental import pallas as pl
from jax.experimental.pallas import tpu as pltpu
from jax.sharding import PartitionSpec as P

SWEEPS = 3
F32 = jnp.float32
LANES = 128
MAP_ROWS = 48
WALL_ROWS = 16
FLOW_ROWS = 16
END_ROWS = 8
VMEM_LIMIT = 16 * 1024 * 1024


def call(kernel, outs, scratch, smem, args, name, flops=1000000):
    specs = [
        pl.BlockSpec(memory_space=pltpu.SMEM if i in smem else pltpu.VMEM)
        for i in range(len(args))
    ]
    moved = sum(a.size * a.dtype.itemsize for a in list(args) + list(outs))
    return pl.pallas_call(
        kernel,
        out_shape=outs,
        in_specs=specs,
        out_specs=[pl.BlockSpec(memory_space=pltpu.VMEM) for _ in outs],
        scratch_shapes=scratch,
        name=name,
        cost_estimate=pl.CostEstimate(flops=flops, bytes_accessed=moved, transcendentals=0),
        compiler_params=pltpu.CompilerParams(vmem_limit_bytes=VMEM_LIMIT),
    )(*args)


def shaped(*shape, dtype=F32):
    return jax.ShapeDtypeStruct(shape, dtype)


def wall_parts_kernel(place_ref, amplitude_ref, patch_ref, modes_ref, columns_ref, mask_ref, out_ref, sums):
    own_modes = modes_ref.shape[0]
    count = modes_ref.shape[2]
    parts = out_ref.shape[0] // WALL_ROWS
    base = place_ref[0] * own_modes
    row, half = owned(place_ref)

    def one(block, carry):
        rows = pl.ds(pl.multiple_of(block * 16, 16), 16)
        target = pl.ds(pl.multiple_of(block * 16 + 8, 8), 16)
        patch = columns_ref[rows, :]
        weights = [
            jnp.where(patch == patch_ref[base + m], amplitude_ref[base + m], 0.0)
            for m in range(own_modes)
        ]
        for c in range(3):
            total = weights[0] * modes_ref[0, c, rows, :].astype(F32)
            for m in range(1, own_modes):
                total = total + weights[m] * modes_ref[m, c, rows, :].astype(F32)
            sums[2 * c, target, :] = total[:, :LANES]
            sums[2 * c + 1, target, :] = total[:, LANES:]
        return carry

    lax.fori_loop(0, count // 16, one, 0)
    for c in range(6):
        sums[c, 0:8, :] = sums[c, count : count + 8, :]
        sums[c, count + 8 : count + 16, :] = sums[c, 8:16, :]

    def put(place, value):
        out_ref[pl.ds(place, parts, stride=WALL_ROWS), :] = value

    for c in range(3):
        for step in range(3):
            put(3 * step + c, sums[2 * c + half, pl.ds(7 + row + step, parts, stride=8), :])
        put(9 + c, sums[2 * c + 1 - half, pl.ds(8 + row, parts, stride=8), :])
    mask = jnp.where(half == 0, mask_ref[:, :LANES], mask_ref[:, LANES:]).astype(F32)
    put(12, jnp.broadcast_to(mask[0:1], (parts, LANES)))
    put(13, jnp.broadcast_to(mask[7:8], (parts, LANES)))
    put(14, jnp.zeros((parts, LANES), F32))
    put(15, jnp.zeros((parts, LANES), F32))


def owned(place_ref):
    return lax.rem(place_ref[1], 8), lax.div(place_ref[1], 8)


def links_of(place_ref, coupling_ref, offsets_ref):
    cells = coupling_ref.shape[0]
    cut = offsets_ref[...] - place_ref[1] * cells

    def link(k):
        return jnp.where(cut == k, 0.0, coupling_ref[k])

    return link


def product(pivot_ref, k, vector):
    return [
        pivot_ref[k, 3 * a] * vector[0]
        + pivot_ref[k, 3 * a + 1] * vector[1]
        + pivot_ref[k, 3 * a + 2] * vector[2]
        for a in range(3)
    ]


def put_lines(out_ref, row, stride, value):
    for half in range(value.shape[1] // LANES):
        out_ref[pl.ds(half * 8 * stride + row, 8, stride=stride), :] = value[
            :, half * LANES : (half + 1) * LANES
        ]


def get_lines(in_ref, row, stride, width):
    return jnp.concatenate(
        [
            in_ref[pl.ds(half * 8 * stride + row, 8, stride=stride), :]
            for half in range(width // LANES)
        ],
        axis=1,
    )


def blend_of(depth, place_ref, cells, k):
    return 1.0 - (place_ref[1] * cells + k).astype(F32) * (1.0 / depth)


def maps_kernel(depth, place_ref, pivot_ref, coupling_ref, offsets_ref, stiff_ref, out_ref, prefix, driven):
    cells = pivot_ref.shape[0]
    link = links_of(place_ref, coupling_ref, offsets_ref)
    first = link(0)

    def source(k, j):
        weight = stiff_ref[k] * blend_of(depth, place_ref, cells, k)
        return [pivot_ref[k, 3 * a + j] * weight for a in range(3)]

    for j in range(3):
        column = [pivot_ref[0, 3 * a + j] * first for a in range(3)]
        forced = source(0, j)
        for a in range(3):
            prefix[0, a] = column[a]
            driven[0, a] = forced[a]
        for k in range(1, cells):
            here = link(k)
            column = product(pivot_ref, k, [here * v for v in column])
            added = source(k, j)
            forced = product(pivot_ref, k, [here * v for v in forced])
            forced = [forced[a] + added[a] for a in range(3)]
            for a in range(3):
                prefix[k, a] = column[a]
                driven[k, a] = forced[a]
        for a in range(3):
            put_lines(out_ref, 3 * a + j, MAP_ROWS, column[a])
            put_lines(out_ref, 27 + 3 * a + j, MAP_ROWS, forced[a])
        upper = [pivot_ref[cells - 1, 3 * a + j] for a in range(3)]
        for k in range(cells - 2, -1, -1):
            above = link(k + 1)
            column = product(pivot_ref, k, [above * v for v in column])
            column = [column[a] + prefix[k, a] for a in range(3)]
            forced = product(pivot_ref, k, [above * v for v in forced])
            forced = [forced[a] + driven[k, a] for a in range(3)]
            upper = product(pivot_ref, k, [above * v for v in upper])
        for a in range(3):
            put_lines(out_ref, 9 + 3 * a + j, MAP_ROWS, first * upper[a])
            put_lines(out_ref, 18 + 3 * a + j, MAP_ROWS, first * column[a])
            put_lines(out_ref, 36 + 3 * a + j, MAP_ROWS, first * forced[a])
    blank = jnp.zeros_like(first)
    for a in range(45, MAP_ROWS):
        put_lines(out_ref, a, MAP_ROWS, blank)


def local_ends(pivot_ref, link, right_ref, values, out_ref):
    cells = pivot_ref.shape[0]
    for k in range(cells):
        state = [right_ref[k, b] for b in range(3)] if k == 0 else [
            right_ref[k, b] + link(k) * state[b] for b in range(3)
        ]
        state = product(pivot_ref, k, state)
        for b in range(3):
            values[k, b] = state[b]
    for b in range(3):
        put_lines(out_ref, b, END_ROWS, state[b])
    for k in range(cells - 2, -1, -1):
        above = link(k + 1)
        lifted = product(pivot_ref, k, [above * v for v in state])
        state = [values[k, b] + lifted[b] for b in range(3)]
    first = link(0)
    for b in range(3):
        put_lines(out_ref, 3 + b, END_ROWS, first * state[b])
    blank = jnp.zeros_like(first)
    for b in range(6, END_ROWS):
        put_lines(out_ref, b, END_ROWS, blank)


def around(value, low, high):
    rows = lax.broadcasted_iota(jnp.int32, value.shape, 0)
    columns = lax.broadcasted_iota(jnp.int32, value.shape, 1)
    height, width = value.shape
    below = jnp.where(rows == 0, low, pltpu.roll(value, 1, 0))
    above = jnp.where(rows == height - 1, high, pltpu.roll(value, height - 1, 0))
    left = jnp.where(columns == 0, 0.0, pltpu.roll(value, 1, 1))
    right = jnp.where(columns == width - 1, 0.0, pltpu.roll(value, width - 1, 1))
    return (below + above) + (left + right)


def next_kernel(place_ref, shape_ref, outer_ref, inner_ref, pivot_ref, coupling_ref, offsets_ref,
                stiff_ref, right_ref, out_ref, values, low_rows, high_rows):
    cells = pivot_ref.shape[0]
    even = lax.rem(place_ref[0], 2) == 0
    inner, outer = inner_ref[...].astype(F32), outer_ref[...].astype(F32)
    low_rows[...] = jnp.where(even, outer, inner)
    high_rows[...] = jnp.where(even, inner, outer)
    for k in range(cells):
        for c in range(3):
            row = 3 * k + c
            summed = around(
                shape_ref[k, c], low_rows[row : row + 1, :], high_rows[row : row + 1, :]
            )
            right_ref[k, c] = stiff_ref[k] * summed
    link = links_of(place_ref, coupling_ref, offsets_ref)
    local_ends(pivot_ref, link, right_ref, values, out_ref)


def row_of(ref, row):
    return ref[row : row + 1, :]


def apply_map(maps_ref, base, vector):
    return [
        row_of(maps_ref, base + 3 * a) * vector[0]
        + row_of(maps_ref, base + 3 * a + 1) * vector[1]
        + row_of(maps_ref, base + 3 * a + 2) * vector[2]
        for a in range(3)
    ]


def chain(maps_ref, ends, wall, out_ref, stride):
    places = maps_ref.shape[0] // MAP_ROWS
    state = wall
    tops = []
    for place in range(places):
        base = place * MAP_ROWS
        end, top = ends(place)
        for c in range(3):
            out_ref[place * stride + c : place * stride + c + 1, :] = state[c]
        reflected = apply_map(maps_ref, base + 18, state)
        tops.append([top[c] + reflected[c] for c in range(3)])
        moved = apply_map(maps_ref, base, state)
        state = [end[c] + moved[c] for c in range(3)]
    state = [jnp.zeros((1, LANES), F32)] * 3
    for place in range(places - 1, -1, -1):
        for c in range(3):
            out_ref[place * stride + 3 + c : place * stride + 4 + c, :] = state[c]
        moved = apply_map(maps_ref, place * MAP_ROWS + 9, state)
        state = [tops[place][c] + moved[c] for c in range(3)]


def first_chain_kernel(place_ref, walls_ref, maps_ref, mask_ref, out_ref, wall_ref, sums, masks):
    parts = walls_ref.shape[0] // WALL_ROWS
    places = maps_ref.shape[0] // MAP_ROWS
    row, half = owned(place_ref)
    total = walls_ref[0:WALL_ROWS, :]
    for s in range(1, parts):
        total = total + walls_ref[WALL_ROWS * s : WALL_ROWS * (s + 1), :]
    sums[...] = total
    mask = mask_ref[...].astype(F32)
    masks[0, 8:16, :] = mask[:, :LANES]
    masks[1, 8:16, :] = mask[:, LANES:]
    below = lax.rem(place_ref[0] + parts - 1, parts)
    above = lax.rem(place_ref[0] + 1, parts)
    masks[half, 7:8, :] = walls_ref[pl.ds(below * WALL_ROWS + 13, 1), :]
    masks[half, 16:17, :] = walls_ref[pl.ds(above * WALL_ROWS + 12, 1), :]
    low_mask = masks[half, pl.ds(7 + row, 1), :]
    own_mask = masks[half, pl.ds(8 + row, 1), :]
    high_mask = masks[half, pl.ds(9 + row, 1), :]
    other_mask = masks[1 - half, pl.ds(8 + row, 1), :]
    lane = lax.broadcasted_iota(jnp.int32, (1, LANES), 1)
    wall, around_wall = [], []
    for c in range(3):
        own = row_of(sums, 3 + c) * own_mask
        other = row_of(sums, 9 + c) * other_mask
        left_edge = jnp.where(half == 1, pltpu.roll(other, 1, 1), 0.0)
        right_edge = jnp.where(half == 0, pltpu.roll(other, LANES - 1, 1), 0.0)
        left = jnp.where(lane == 0, left_edge, pltpu.roll(own, 1, 1))
        right = jnp.where(lane == LANES - 1, right_edge, pltpu.roll(own, LANES - 1, 1))
        ends = row_of(sums, c) * low_mask + row_of(sums, 6 + c) * high_mask
        wall.append(own)
        around_wall.append(ends + (left + right))
        wall_ref[c : c + 1, :] = own

    def ends_at(place):
        base = place * MAP_ROWS
        return (
            apply_map(maps_ref, base + 27, around_wall),
            apply_map(maps_ref, base + 36, around_wall),
        )

    chain(maps_ref, ends_at, wall, out_ref, FLOW_ROWS)
    for place in range(places):
        base = place * FLOW_ROWS
        for c in range(3):
            out_ref[base + 6 + c : base + 7 + c, :] = around_wall[c]
        out_ref[base + 9 : base + 16, :] = jnp.zeros((7, LANES), F32)


def next_chain_kernel(maps_ref, ends_ref, wall_ref, out_ref):
    def ends_at(place):
        base = place * END_ROWS
        return (
            [row_of(ends_ref, base + c) for c in range(3)],
            [row_of(ends_ref, base + 3 + c) for c in range(3)],
        )

    chain(maps_ref, ends_at, [row_of(wall_ref, c) for c in range(3)], out_ref, END_ROWS)
    for place in range(ends_ref.shape[0] // END_ROWS):
        base = place * END_ROWS
        out_ref[base + 6 : base + 8, :] = jnp.zeros((2, LANES), F32)


def solve(place_ref, flows_ref, stride, right, pivot_ref, coupling_ref, offsets_ref, shape_ref, edges, values):
    cells = pivot_ref.shape[0]
    width = shape_ref.shape[3]
    link = links_of(place_ref, coupling_ref, offsets_ref)
    state = [get_lines(flows_ref, c, stride, width) for c in range(3)]
    for k in range(cells):
        here = link(k)
        given = right(k)
        state = product(pivot_ref, k, [given[b] + here * state[b] for b in range(3)])
        for b in range(3):
            values[k, b] = state[b]
    lifted = [get_lines(flows_ref, 3 + c, stride, width) for c in range(3)]
    for k in range(cells - 1, -1, -1):
        lifted = product(pivot_ref, k, lifted)
        state = [values[k, b] + lifted[b] for b in range(3)]
        for b in range(3):
            shape_ref[k, b] = state[b]
            if edges:
                row = 3 * k + b
                edges[2][row : row + 1, :] = state[b][0:1]
                edges[3][row : row + 1, :] = state[b][7:8]
        if k:
            here = link(k)
            lifted = [here * v for v in state]
    if edges:
        even = lax.rem(place_ref[0], 2) == 0
        first, final = edges[2][...], edges[3][...]
        edges[0][...] = jnp.where(even, final, first).astype(jnp.bfloat16)
        edges[1][...] = jnp.where(even, first, final).astype(jnp.bfloat16)


def first_solve_kernel(depth, place_ref, flows_ref, stiff_ref, pivot_ref, coupling_ref, offsets_ref,
                       shape_ref, inner_ref, outer_ref, values, first_rows, last_rows):
    cells = pivot_ref.shape[0]
    width = shape_ref.shape[3]
    around_wall = [get_lines(flows_ref, 6 + c, FLOW_ROWS, width) for c in range(3)]

    def right(k):
        weight = stiff_ref[k] * blend_of(depth, place_ref, cells, k)
        return [weight * v for v in around_wall]

    edges = (inner_ref, outer_ref, first_rows, last_rows)
    solve(place_ref, flows_ref, FLOW_ROWS, right, pivot_ref, coupling_ref, offsets_ref, shape_ref, edges, values)


def solve_kernel(place_ref, flows_ref, right_ref, pivot_ref, coupling_ref, offsets_ref, shape_ref, *rest):
    def right(k):
        return [right_ref[k, b] for b in range(3)]

    edges = (rest[0], rest[1], rest[3], rest[4]) if len(rest) > 1 else ()
    values = rest[2] if edges else rest[0]
    solve(place_ref, flows_ref, END_ROWS, right, pivot_ref, coupling_ref, offsets_ref, shape_ref, edges, values)


def per_device(
    mode_shapes,
    amplitude,
    mode_patch,
    column_patch,
    wall_mask,
    offsets,
    coupling,
    pivot_inv,
    stiffness,
):
    rows, width = wall_mask.shape
    cells = coupling.shape[0]
    surf, norm = lax.axis_size("surf"), lax.axis_size("norm")
    place = jnp.stack([lax.axis_index("surf"), lax.axis_index("norm")]).astype(jnp.int32)
    modes = jnp.transpose(mode_shapes, (0, 2, 1, 3))
    pivots = jnp.transpose(pivot_inv, (0, 2, 1, 3))
    cube = shaped(cells, 3, rows, width)
    scratch = pltpu.VMEM((cells, 3, rows, width), F32)
    edge = shaped(cells * 3, width, dtype=jnp.bfloat16)
    edge_scratch = pltpu.VMEM((cells * 3, width), F32)
    depth = cells * norm

    def swapped(block, axis, count):
        block = block.reshape((count, block.shape[0] // count) + block.shape[1:])
        block = lax.all_to_all(block, axis, 0, 0, tiled=True)
        return block.reshape((-1,) + block.shape[2:])

    (maps,) = call(
        functools.partial(maps_kernel, depth),
        [shaped(norm * MAP_ROWS, LANES)],
        [scratch, scratch],
        (0,),
        (place, pivots, coupling, offsets, stiffness),
        "maps",
    )
    maps = swapped(maps, "norm", norm)
    (walls,) = call(
        wall_parts_kernel,
        [shaped(surf * WALL_ROWS, LANES)],
        [pltpu.VMEM((6, mode_shapes.shape[1] + 16, LANES), F32)],
        (0, 1, 2),
        (place, amplitude, mode_patch, modes, column_patch, wall_mask),
        "wall_parts",
    )
    walls, maps = lax.optimization_barrier((walls, maps))
    walls = swapped(walls, "surf", surf)
    flows, wall = call(
        first_chain_kernel,
        [shaped(norm * FLOW_ROWS, LANES), shaped(8, LANES)],
        [pltpu.VMEM((WALL_ROWS, LANES), F32), pltpu.VMEM((2, 24, LANES), F32)],
        (0,),
        (place, walls, maps, wall_mask),
        "first_chain",
    )
    flows = swapped(flows, "norm", norm)
    local = (pivots, coupling, offsets)
    edges = [scratch, edge_scratch, edge_scratch]
    shape, inner, outer = call(
        functools.partial(first_solve_kernel, depth),
        [cube, edge, edge],
        edges,
        (0,),
        (place, flows, stiffness) + local,
        "first_solve",
    )
    for sweep in range(1, SWEEPS):
        outer = lax.ppermute(
            outer, "surf", [(i, (i - 1 + 2 * (i % 2)) % surf) for i in range(surf)]
        )
        inner = lax.ppermute(inner, "surf", [(i, i + 1 - 2 * (i % 2)) for i in range(surf)])
        right, ends = call(
            next_kernel,
            [cube, shaped(norm * END_ROWS, LANES)],
            edges,
            (0,),
            (place, shape, outer, inner) + local + (stiffness,),
            "next_ends",
        )
        ends = swapped(ends, "norm", norm)
        (flows,) = call(
            next_chain_kernel, [shaped(norm * END_ROWS, LANES)], [], (), (maps, ends, wall), "chain"
        )
        flows = swapped(flows, "norm", norm)
        last = sweep == SWEEPS - 1
        solved = call(
            solve_kernel,
            [cube] if last else [cube, edge, edge],
            [scratch] if last else edges,
            (0,),
            (place, flows, right) + local,
            "solve",
        )
        if not last:
            shape, inner, outer = solved
    return jnp.transpose(solved[0], (0, 2, 1, 3))


def solution(mesh):
    return jax.shard_map(
        per_device,
        mesh=mesh,
        in_specs=(
            P("surf", None, None, None),
            P(),
            P(),
            P(),
            P("surf", None),
            P("surf", None),
            P("norm", "surf", None),
            P("norm", "surf", None, None),
            P("norm", "surf", None),
        ),
        out_specs=P("norm", "surf", None, None),
        check_vma=False,
    )
```

```python
import functools
import jax
import jax.numpy as jnp
from jax import lax
from jax.experimental import pallas as pl
from jax.experimental.pallas import tpu as pltpu
from jax.sharding import PartitionSpec as P

SWEEPS = 3
F32 = jnp.float32
LANES = 128
MAP_ROWS = 48
WALL_ROWS = 16
FLOW_ROWS = 16
END_ROWS = 8
VMEM_LIMIT = 16 * 1024 * 1024
VMEM_FRONT = 60 * 1024 * 1024


def call(kernel, outs, scratch, args, name, far=False):
    space = pltpu.HBM if far else pltpu.VMEM
    moved = sum(a.size * a.dtype.itemsize for a in list(args) + list(outs))

    def body(*refs):
        kernel((lax.axis_index("surf"), lax.axis_index("norm")), *refs)

    return pl.pallas_call(
        body,
        out_shape=outs,
        in_specs=[pl.BlockSpec(memory_space=space) for _ in args],
        out_specs=[pl.BlockSpec(memory_space=pltpu.VMEM) for _ in outs],
        scratch_shapes=scratch,
        name=name,
        cost_estimate=pl.CostEstimate(flops=1000000, bytes_accessed=moved, transcendentals=0),
        compiler_params=pltpu.CompilerParams(vmem_limit_bytes=VMEM_FRONT if far else VMEM_LIMIT),
    )(*args)


def shaped(*shape, dtype=F32):
    return jax.ShapeDtypeStruct(shape, dtype)


def wall_parts(mine, amplitude_ref, patch_ref, modes_ref, columns_ref, mask_ref, keep_ref, send_refs,
               sums, blocks):
    own_modes = modes_ref.shape[0]
    count = modes_ref.shape[2]
    parts = blocks.shape[0] // WALL_ROWS
    base = mine[0] * own_modes
    row, half = owned(mine)

    def one(block, carry):
        rows = pl.ds(pl.multiple_of(block * 16, 16), 16)
        target = pl.ds(pl.multiple_of(block * 16 + 8, 8), 16)
        patch = columns_ref[rows, :]
        weights = [
            jnp.where(patch == patch_ref[base + m], amplitude_ref[base + m], 0.0)
            for m in range(own_modes)
        ]
        for c in range(3):
            total = weights[0] * modes_ref[0, c, rows, :].astype(F32)
            for m in range(1, own_modes):
                total = total + weights[m] * modes_ref[m, c, rows, :].astype(F32)
            sums[2 * c, target, :] = total[:, :LANES]
            sums[2 * c + 1, target, :] = total[:, LANES:]
        return carry

    lax.fori_loop(0, count // 16, one, 0)
    for c in range(6):
        sums[c, 0:8, :] = sums[c, count : count + 8, :]
        sums[c, count + 8 : count + 16, :] = sums[c, 8:16, :]

    def put(place, from_ref, start):
        for odd in range(2):
            blocks[pl.ds(odd * (parts // 2) * WALL_ROWS + place, parts // 2, stride=WALL_ROWS), :] = (
                from_ref[pl.ds(start + 8 * odd, parts // 2, stride=16), :]
            )

    for c in range(3):
        for step in range(3):
            put(3 * step + c, sums.at[2 * c + half], 7 + row + step)
        put(9 + c, sums.at[2 * c + 1 - half], 8 + row)
    blank = jnp.zeros((parts, LANES), F32)
    for place in range(12, 16):
        blocks[pl.ds(place, parts, stride=WALL_ROWS), :] = blank
    mask = jnp.where(half == 0, mask_ref[:, :LANES], mask_ref[:, LANES:]).astype(F32)
    for step, place, edge in ((1, 12, 7), (parts - 1, 13, 0)):
        target = lax.rem(mine[0] + step, parts)
        order = lax.rem(target, 2) * (parts // 2) + lax.div(target, 2)
        blocks[pl.ds(order * WALL_ROWS + place, 1), :] = mask[edge : edge + 1]
    parted(mine, blocks, keep_ref, send_refs, 0)


def parted(mine, blocks, keep_ref, send_refs, shift):
    rows = keep_ref.shape[0]
    radix = len(send_refs) + 1
    own = lax.rem(lax.shift_right_logical(mine[0], shift), radix)
    for step, ref in enumerate([keep_ref] + list(send_refs)):
        group = lax.bitwise_xor(own, step)
        ref[...] = blocks[pl.ds(pl.multiple_of(group * rows, 16), rows), :]


def wall_sum_kernel(shift, radix, mine, keep_ref, *rest):
    got, next_ref, send_refs, blocks = rest[:-radix - 1], rest[-radix - 1], rest[-radix:-1], rest[-1]
    total = keep_ref[...]
    for ref in got:
        total = total + ref[...]
    blocks[...] = total
    parted(mine, blocks, next_ref, send_refs, shift)


def owned(mine):
    return lax.rem(mine[1], 8), lax.div(mine[1], 8)


def links_of(mine, coupling_ref, offsets_ref):
    cells = coupling_ref.shape[0]
    cut = offsets_ref[...] - mine[1] * cells

    def link(k):
        return jnp.where(cut == k, 0.0, coupling_ref[k])

    return link


def product(pivot_ref, k, vector):
    return [
        pivot_ref[k, 3 * a] * vector[0]
        + pivot_ref[k, 3 * a + 1] * vector[1]
        + pivot_ref[k, 3 * a + 2] * vector[2]
        for a in range(3)
    ]


def put_lines(out_ref, row, stride, value):
    for half in range(value.shape[1] // LANES):
        out_ref[pl.ds(half * 8 * stride + row, 8, stride=stride), :] = value[
            :, half * LANES : (half + 1) * LANES
        ]


def get_lines(in_ref, row, stride, width):
    return jnp.concatenate(
        [
            in_ref[pl.ds(half * 8 * stride + row, 8, stride=stride), :]
            for half in range(width // LANES)
        ],
        axis=1,
    )


def blend_of(depth, mine, cells, k):
    return 1.0 - (mine[1] * cells + k).astype(F32) * (1.0 / depth)


def segment_maps(depth, arrive, mine, pivot_ref, coupling_ref, offsets_ref, stiff_ref, out_ref, prefix, driven):
    cells = pivot_ref.shape[0]
    link = links_of(mine, coupling_ref, offsets_ref)
    first = link(0)

    def source(k, j):
        weight = stiff_ref[k] * blend_of(depth, mine, cells, k)
        return [pivot_ref[k, 3 * a + j] * weight for a in range(3)]

    for j in range(3):
        if j == 0:
            arrive(0)
        column = [pivot_ref[0, 3 * a + j] * first for a in range(3)]
        forced = source(0, j)
        for a in range(3):
            prefix[0, a] = column[a]
            driven[0, a] = forced[a]
        for k in range(1, cells):
            if j == 0:
                arrive(k)
            here = link(k)
            column = product(pivot_ref, k, [here * v for v in column])
            added = source(k, j)
            forced = product(pivot_ref, k, [here * v for v in forced])
            forced = [forced[a] + added[a] for a in range(3)]
            for a in range(3):
                prefix[k, a] = column[a]
                driven[k, a] = forced[a]
        for a in range(3):
            put_lines(out_ref, 3 * a + j, MAP_ROWS, column[a])
            put_lines(out_ref, 27 + 3 * a + j, MAP_ROWS, forced[a])
        upper = [pivot_ref[cells - 1, 3 * a + j] for a in range(3)]
        for k in range(cells - 2, -1, -1):
            above = link(k + 1)
            column = product(pivot_ref, k, [above * v for v in column])
            column = [column[a] + prefix[k, a] for a in range(3)]
            forced = product(pivot_ref, k, [above * v for v in forced])
            forced = [forced[a] + driven[k, a] for a in range(3)]
            upper = product(pivot_ref, k, [above * v for v in upper])
        for a in range(3):
            put_lines(out_ref, 9 + 3 * a + j, MAP_ROWS, first * upper[a])
            put_lines(out_ref, 18 + 3 * a + j, MAP_ROWS, first * column[a])
            put_lines(out_ref, 36 + 3 * a + j, MAP_ROWS, first * forced[a])
    blank = jnp.zeros_like(first)
    for a in range(45, MAP_ROWS):
        put_lines(out_ref, a, MAP_ROWS, blank)


def front_kernel(depth, mine, *rest):
    far, rest = rest[:9], rest[9:]
    (maps_ref, keep_ref, send_ref), rest = rest[:3], rest[3:]
    near, (prefix, driven, sums, blocks, arrived, pieces) = rest[:9], rest[9:]
    amplitude, patch, modes, columns, mask, pivot, coupling, offsets, stiff = near
    cells = pivot.shape[0]
    step = cells // 4
    parts = [
        pltpu.make_async_copy(
            far[5].at[step * i : step * (i + 1)], pivot.at[step * i : step * (i + 1)], pieces.at[i]
        )
        for i in range(4)
    ]
    whole = {i: pltpu.make_async_copy(far[i], near[i], arrived.at[i]) for i in range(9) if i != 5}
    for copy in [whole[6], whole[7], whole[8]] + parts + [whole[i] for i in range(5)]:
        copy.start()
    for i in (6, 7, 8):
        whole[i].wait()

    def arrive(k):
        if k % step == 0:
            parts[k // step].wait()

    segment_maps(depth, arrive, mine, pivot, coupling, offsets, stiff, maps_ref, prefix, driven)
    for i in range(5):
        whole[i].wait()
    wall_parts(mine, amplitude, patch, modes, columns, mask, keep_ref, [send_ref], sums, blocks)


def local_ends(pivot_ref, link, right_ref, values, out_ref):
    cells = pivot_ref.shape[0]
    for k in range(cells):
        state = [right_ref[k, b] for b in range(3)] if k == 0 else [
            right_ref[k, b] + link(k) * state[b] for b in range(3)
        ]
        state = product(pivot_ref, k, state)
        for b in range(3):
            values[k, b] = state[b]
    for b in range(3):
        put_lines(out_ref, b, END_ROWS, state[b])
    for k in range(cells - 2, -1, -1):
        above = link(k + 1)
        lifted = product(pivot_ref, k, [above * v for v in state])
        state = [values[k, b] + lifted[b] for b in range(3)]
    first = link(0)
    for b in range(3):
        put_lines(out_ref, 3 + b, END_ROWS, first * state[b])
    blank = jnp.zeros_like(first)
    for b in range(6, END_ROWS):
        put_lines(out_ref, b, END_ROWS, blank)


def around(value, low, high):
    rows = lax.broadcasted_iota(jnp.int32, value.shape, 0)
    columns = lax.broadcasted_iota(jnp.int32, value.shape, 1)
    height, width = value.shape
    below = jnp.where(rows == 0, low, pltpu.roll(value, 1, 0))
    above = jnp.where(rows == height - 1, high, pltpu.roll(value, height - 1, 0))
    left = jnp.where(columns == 0, 0.0, pltpu.roll(value, 1, 1))
    right = jnp.where(columns == width - 1, 0.0, pltpu.roll(value, width - 1, 1))
    return (below + above) + (left + right)


def next_kernel(mine, shape_ref, outer_ref, inner_ref, pivot_ref, coupling_ref, offsets_ref,
                stiff_ref, right_ref, out_ref, values, low_rows, high_rows):
    cells = pivot_ref.shape[0]
    even = lax.rem(mine[0], 2) == 0
    inner, outer = inner_ref[...].astype(F32), outer_ref[...].astype(F32)
    low_rows[...] = jnp.where(even, outer, inner)
    high_rows[...] = jnp.where(even, inner, outer)
    for k in range(cells):
        for c in range(3):
            row = 3 * k + c
            summed = around(
                shape_ref[k, c], low_rows[row : row + 1, :], high_rows[row : row + 1, :]
            )
            right_ref[k, c] = stiff_ref[k] * summed
    link = links_of(mine, coupling_ref, offsets_ref)
    local_ends(pivot_ref, link, right_ref, values, out_ref)


def row_of(ref, row):
    return ref[row : row + 1, :]


def apply_map(maps_ref, base, vector):
    return [
        row_of(maps_ref, base + 3 * a) * vector[0]
        + row_of(maps_ref, base + 3 * a + 1) * vector[1]
        + row_of(maps_ref, base + 3 * a + 2) * vector[2]
        for a in range(3)
    ]


def chain(maps_ref, ends, wall, out_ref, stride):
    places = maps_ref.shape[0] // MAP_ROWS
    state = wall
    tops = []
    for place in range(places):
        base = place * MAP_ROWS
        end, top = ends(place)
        for c in range(3):
            out_ref[place * stride + c : place * stride + c + 1, :] = state[c]
        reflected = apply_map(maps_ref, base + 18, state)
        tops.append([top[c] + reflected[c] for c in range(3)])
        moved = apply_map(maps_ref, base, state)
        state = [end[c] + moved[c] for c in range(3)]
    state = [jnp.zeros((1, LANES), F32)] * 3
    for place in range(places - 1, -1, -1):
        for c in range(3):
            out_ref[place * stride + 3 + c : place * stride + 4 + c, :] = state[c]
        moved = apply_map(maps_ref, place * MAP_ROWS + 9, state)
        state = [tops[place][c] + moved[c] for c in range(3)]


def first_chain_kernel(mine, maps_ref, mask_ref, *rest):
    given, (out_ref, wall_ref, sums, masks) = rest[:-4], rest[-4:]
    places = maps_ref.shape[0] // MAP_ROWS
    row, half = owned(mine)
    total = given[0][...]
    for ref in given[1:]:
        total = total + ref[...]
    sums[...] = total
    mask = mask_ref[...].astype(F32)
    masks[0, 8:16, :] = mask[:, :LANES]
    masks[1, 8:16, :] = mask[:, LANES:]
    masks[half, 7:8, :] = row_of(sums, 12)
    masks[half, 16:17, :] = row_of(sums, 13)
    low_mask = masks[half, pl.ds(7 + row, 1), :]
    own_mask = masks[half, pl.ds(8 + row, 1), :]
    high_mask = masks[half, pl.ds(9 + row, 1), :]
    other_mask = masks[1 - half, pl.ds(8 + row, 1), :]
    lane = lax.broadcasted_iota(jnp.int32, (1, LANES), 1)
    wall, around_wall = [], []
    for c in range(3):
        own = row_of(sums, 3 + c) * own_mask
        other = row_of(sums, 9 + c) * other_mask
        left_edge = jnp.where(half == 1, pltpu.roll(other, 1, 1), 0.0)
        right_edge = jnp.where(half == 0, pltpu.roll(other, LANES - 1, 1), 0.0)
        left = jnp.where(lane == 0, left_edge, pltpu.roll(own, 1, 1))
        right = jnp.where(lane == LANES - 1, right_edge, pltpu.roll(own, LANES - 1, 1))
        ends = row_of(sums, c) * low_mask + row_of(sums, 6 + c) * high_mask
        wall.append(own)
        around_wall.append(ends + (left + right))
        wall_ref[c : c + 1, :] = own

    def ends_at(place):
        base = place * MAP_ROWS
        return (
            apply_map(maps_ref, base + 27, around_wall),
            apply_map(maps_ref, base + 36, around_wall),
        )

    chain(maps_ref, ends_at, wall, out_ref, FLOW_ROWS)
    for place in range(places):
        base = place * FLOW_ROWS
        for c in range(3):
            out_ref[base + 6 + c : base + 7 + c, :] = around_wall[c]
        out_ref[base + 9 : base + 16, :] = jnp.zeros((7, LANES), F32)


def next_chain_kernel(mine, maps_ref, ends_ref, wall_ref, out_ref):
    def ends_at(place):
        base = place * END_ROWS
        return (
            [row_of(ends_ref, base + c) for c in range(3)],
            [row_of(ends_ref, base + 3 + c) for c in range(3)],
        )

    chain(maps_ref, ends_at, [row_of(wall_ref, c) for c in range(3)], out_ref, END_ROWS)
    for place in range(ends_ref.shape[0] // END_ROWS):
        base = place * END_ROWS
        out_ref[base + 6 : base + 8, :] = jnp.zeros((2, LANES), F32)


def solve(mine, flows_ref, stride, right, pivot_ref, coupling_ref, offsets_ref, shape_ref, edges, values):
    cells = pivot_ref.shape[0]
    width = shape_ref.shape[3]
    link = links_of(mine, coupling_ref, offsets_ref)
    state = [get_lines(flows_ref, c, stride, width) for c in range(3)]
    for k in range(cells):
        here = link(k)
        given = right(k)
        state = product(pivot_ref, k, [given[b] + here * state[b] for b in range(3)])
        for b in range(3):
            values[k, b] = state[b]
    lifted = [get_lines(flows_ref, 3 + c, stride, width) for c in range(3)]
    for k in range(cells - 1, -1, -1):
        lifted = product(pivot_ref, k, lifted)
        state = [values[k, b] + lifted[b] for b in range(3)]
        for b in range(3):
            shape_ref[k, b] = state[b]
            if edges:
                row = 3 * k + b
                edges[2][row : row + 1, :] = state[b][0:1]
                edges[3][row : row + 1, :] = state[b][7:8]
        if k:
            here = link(k)
            lifted = [here * v for v in state]
    if edges:
        even = lax.rem(mine[0], 2) == 0
        first, final = edges[2][...], edges[3][...]
        edges[0][...] = jnp.where(even, final, first).astype(jnp.bfloat16)
        edges[1][...] = jnp.where(even, first, final).astype(jnp.bfloat16)


def first_solve_kernel(depth, mine, flows_ref, stiff_ref, pivot_ref, coupling_ref, offsets_ref,
                       shape_ref, inner_ref, outer_ref, values, first_rows, last_rows):
    cells = pivot_ref.shape[0]
    width = shape_ref.shape[3]
    around_wall = [get_lines(flows_ref, 6 + c, FLOW_ROWS, width) for c in range(3)]

    def right(k):
        weight = stiff_ref[k] * blend_of(depth, mine, cells, k)
        return [weight * v for v in around_wall]

    edges = (inner_ref, outer_ref, first_rows, last_rows)
    solve(mine, flows_ref, FLOW_ROWS, right, pivot_ref, coupling_ref, offsets_ref, shape_ref, edges, values)


def solve_kernel(mine, flows_ref, right_ref, pivot_ref, coupling_ref, offsets_ref, shape_ref, *rest):
    def right(k):
        return [right_ref[k, b] for b in range(3)]

    edges = (rest[0], rest[1], rest[3], rest[4]) if len(rest) > 1 else ()
    values = rest[2] if edges else rest[0]
    solve(mine, flows_ref, END_ROWS, right, pivot_ref, coupling_ref, offsets_ref, shape_ref, edges, values)


def per_device(
    mode_shapes,
    amplitude,
    mode_patch,
    column_patch,
    wall_mask,
    offsets,
    coupling,
    pivot_inv,
    stiffness,
):
    rows, width = wall_mask.shape
    cells = coupling.shape[0]
    surf, norm = lax.axis_size("surf"), lax.axis_size("norm")
    modes = jnp.transpose(mode_shapes, (0, 2, 1, 3))
    pivots = jnp.transpose(pivot_inv, (0, 2, 1, 3))
    cube = shaped(cells, 3, rows, width)
    scratch = pltpu.VMEM((cells, 3, rows, width), F32)
    edge = shaped(cells * 3, width, dtype=jnp.bfloat16)
    edge_scratch = pltpu.VMEM((cells * 3, width), F32)
    depth = cells * norm

    def swapped(block, axis, count):
        block = block.reshape((count, block.shape[0] // count) + block.shape[1:])
        block = lax.all_to_all(block, axis, 0, 0, tiled=True)
        return block.reshape((-1,) + block.shape[2:])

    size = surf * WALL_ROWS // 2
    given = (amplitude, mode_patch, modes, column_patch, wall_mask, pivots, coupling, offsets, stiffness)
    near = [
        (pltpu.SMEM if a.ndim == 1 else pltpu.VMEM)(a.shape, a.dtype) for a in given
    ]
    maps, keep, send = call(
        functools.partial(front_kernel, depth),
        [shaped(norm * MAP_ROWS, LANES), shaped(size, LANES), shaped(size, LANES)],
        near
        + [
            scratch,
            scratch,
            pltpu.VMEM((6, mode_shapes.shape[1] + 16, LANES), F32),
            pltpu.VMEM((2 * size, LANES), F32),
            pltpu.SemaphoreType.DMA((9,)),
            pltpu.SemaphoreType.DMA((4,)),
        ],
        given,
        "front",
        far=True,
    )
    got = lax.ppermute(send, "surf", [(i, i ^ 1) for i in range(surf)])
    maps, got = lax.optimization_barrier((maps, got))
    maps, got = swapped(maps, "norm", norm), [got]
    for shift in (3, 1):
        size //= 4
        keep, *sends = call(
            functools.partial(wall_sum_kernel, shift, 4),
            [shaped(size, LANES)] * 4,
            [pltpu.VMEM((4 * size, LANES), F32)],
            (keep, *got),
            "wall_sum",
        )
        got = [
            lax.ppermute(part, "surf", [(i, i ^ (step << shift)) for i in range(surf)])
            for step, part in enumerate(sends, 1)
        ]
    flows, wall = call(
        first_chain_kernel,
        [shaped(norm * FLOW_ROWS, LANES), shaped(8, LANES)],
        [pltpu.VMEM((WALL_ROWS, LANES), F32), pltpu.VMEM((2, 24, LANES), F32)],
        (maps, wall_mask, keep, *got),
        "first_chain",
    )
    flows = swapped(flows, "norm", norm)
    local = (pivots, coupling, offsets)
    edges = [scratch, edge_scratch, edge_scratch]
    shape, inner, outer = call(
        functools.partial(first_solve_kernel, depth),
        [cube, edge, edge],
        edges,
        (flows, stiffness) + local,
        "first_solve",
    )
    for sweep in range(1, SWEEPS):
        outer = lax.ppermute(
            outer, "surf", [(i, (i - 1 + 2 * (i % 2)) % surf) for i in range(surf)]
        )
        inner = lax.ppermute(inner, "surf", [(i, i + 1 - 2 * (i % 2)) for i in range(surf)])
        right, ends = call(
            next_kernel,
            [cube, shaped(norm * END_ROWS, LANES)],
            edges,
                (shape, outer, inner) + local + (stiffness,),
            "next_ends",
        )
        ends = swapped(ends, "norm", norm)
        (flows,) = call(
            next_chain_kernel, [shaped(norm * END_ROWS, LANES)], [], (maps, ends, wall), "chain"
        )
        flows = swapped(flows, "norm", norm)
        last = sweep == SWEEPS - 1
        solved = call(
            solve_kernel,
            [cube] if last else [cube, edge, edge],
            [scratch] if last else edges,
                (flows, right) + local,
            "solve",
        )
        if not last:
            shape, inner, outer = solved
    return jnp.transpose(solved[0], (0, 2, 1, 3))


def solution(mesh):
    return jax.shard_map(
        per_device,
        mesh=mesh,
        in_specs=(
            P("surf", None, None, None),
            P(),
            P(),
            P(),
            P("surf", None),
            P("surf", None),
            P("norm", "surf", None),
            P("norm", "surf", None, None),
            P("norm", "surf", None),
        ),
        out_specs=P("norm", "surf", None, None),
        check_vma=False,
    )
```

```python
import functools
import jax
import jax.numpy as jnp
from jax import lax
from jax.experimental import pallas as pl
from jax.experimental.pallas import tpu as pltpu
from jax.sharding import PartitionSpec as P

SWEEPS = 3
F32 = jnp.float32
LANES = 128
MAP_ROWS = 48
WALL_ROWS = 16
FLOW_ROWS = 9
END_ROWS = 8
VMEM_LIMIT = 16 * 1024 * 1024
VMEM_FRONT = 60 * 1024 * 1024


def call(kernel, outs, scratch, args, name, far=False):
    space = pltpu.HBM if far else pltpu.VMEM
    moved = sum(a.size * a.dtype.itemsize for a in list(args) + list(outs))

    def body(*refs):
        kernel((lax.axis_index("surf"), lax.axis_index("norm")), *refs)

    return pl.pallas_call(
        body,
        out_shape=outs,
        in_specs=[pl.BlockSpec(memory_space=space) for _ in args],
        out_specs=[pl.BlockSpec(memory_space=pltpu.VMEM) for _ in outs],
        scratch_shapes=scratch,
        name=name,
        cost_estimate=pl.CostEstimate(flops=1000000, bytes_accessed=moved, transcendentals=0),
        compiler_params=pltpu.CompilerParams(vmem_limit_bytes=VMEM_FRONT if far else VMEM_LIMIT),
    )(*args)


def shaped(*shape, dtype=F32):
    return jax.ShapeDtypeStruct(shape, dtype)


def wall_parts(mine, amplitude_ref, patch_ref, modes_ref, columns_ref, mask_ref, keep_ref, send_ref, sums, blocks):
    own_modes = modes_ref.shape[0]
    count = modes_ref.shape[2]
    parts = blocks.shape[0] // WALL_ROWS
    base = mine[0] * own_modes
    row, half = owned(mine)

    def one(block, carry):
        rows = pl.ds(pl.multiple_of(block * 16, 16), 16)
        target = pl.ds(pl.multiple_of(block * 16 + 8, 8), 16)
        patch = columns_ref[rows, :]
        weights = [
            jnp.where(patch == patch_ref[base + m], amplitude_ref[base + m], 0.0)
            for m in range(own_modes)
        ]
        for c in range(3):
            total = weights[0] * modes_ref[0, c, rows, :].astype(F32)
            for m in range(1, own_modes):
                total = total + weights[m] * modes_ref[m, c, rows, :].astype(F32)
            sums[2 * c, target, :] = total[:, :LANES]
            sums[2 * c + 1, target, :] = total[:, LANES:]
        return carry

    lax.fori_loop(0, count // 16, one, 0)
    for c in range(6):
        sums[c, 0:8, :] = sums[c, count : count + 8, :]
        sums[c, count + 8 : count + 16, :] = sums[c, 8:16, :]

    def put(place, from_ref, start):
        for odd in range(2):
            blocks[pl.ds(odd * (parts // 2) * WALL_ROWS + place, parts // 2, stride=WALL_ROWS), :] = (
                from_ref[pl.ds(start + 8 * odd, parts // 2, stride=16), :]
            )

    for c in range(3):
        for step in range(3):
            put(3 * step + c, sums.at[2 * c + half], 7 + row + step)
        put(9 + c, sums.at[2 * c + 1 - half], 8 + row)
    blank = jnp.zeros((parts, LANES), F32)
    for place in range(12, 16):
        blocks[pl.ds(place, parts, stride=WALL_ROWS), :] = blank
    mask = jnp.where(half == 0, mask_ref[:, :LANES], mask_ref[:, LANES:]).astype(F32)
    for step, place, edge in ((1, 12, 7), (parts - 1, 13, 0)):
        target = lax.rem(mine[0] + step, parts)
        order = lax.rem(target, 2) * (parts // 2) + lax.div(target, 2)
        blocks[pl.ds(order * WALL_ROWS + place, 1), :] = mask[edge : edge + 1]
    side = lax.rem(mine[0], 2)
    half_rows = keep_ref.shape[0]
    keep_ref[...] = blocks[pl.ds(pl.multiple_of(side * half_rows, 16), half_rows), :]
    send_ref[...] = blocks[pl.ds(pl.multiple_of((1 - side) * half_rows, 16), half_rows), :]


def wall_sum_kernel(shift, mine, keep_ref, got_ref, next_ref, send_ref, blocks):
    blocks[...] = keep_ref[...] + got_ref[...]
    rows = keep_ref.shape[0] // 4
    own = lax.rem(lax.shift_right_logical(mine[0], shift), 4)
    for ref, steps in ((next_ref, (0, 3)), (send_ref, (1, 2))):
        for i, step in enumerate(steps):
            start = pl.multiple_of(lax.bitwise_xor(own, step) * rows, 16)
            ref[i * rows : (i + 1) * rows, :] = blocks[pl.ds(start, rows), :]


def wall_half_kernel(mine, keep_ref, got_ref, next_ref, send_ref):
    rows = next_ref.shape[0]
    next_ref[...] = keep_ref[:rows] + got_ref[:rows]
    send_ref[...] = keep_ref[rows:] + got_ref[rows:]


def owned(mine):
    return lax.rem(mine[1], 8), lax.div(mine[1], 8)


def links_of(mine, coupling_ref, offsets_ref):
    cells = coupling_ref.shape[0]
    cut = offsets_ref[...] - mine[1] * cells

    def link(k):
        return jnp.where(cut == k, 0.0, coupling_ref[k])

    return link


def product(pivot_ref, k, vector):
    return [
        pivot_ref[k, 3 * a] * vector[0]
        + pivot_ref[k, 3 * a + 1] * vector[1]
        + pivot_ref[k, 3 * a + 2] * vector[2]
        for a in range(3)
    ]


def put_lines(out_ref, row, stride, value):
    for half in range(value.shape[1] // LANES):
        out_ref[pl.ds(half * 8 * stride + row, 8, stride=stride), :] = value[
            :, half * LANES : (half + 1) * LANES
        ]


def get_lines(in_ref, row, stride, width):
    return jnp.concatenate(
        [
            in_ref[pl.ds(half * 8 * stride + row, 8, stride=stride), :]
            for half in range(width // LANES)
        ],
        axis=1,
    )


def blend_of(depth, mine, cells, k):
    return 1.0 - (mine[1] * cells + k).astype(F32) * (1.0 / depth)


def maps_kernel(depth, mine, pivot_ref, coupling_ref, offsets_ref, stiff_ref, out_ref, prefix, driven):
    cells = pivot_ref.shape[0]
    link = links_of(mine, coupling_ref, offsets_ref)
    first = link(0)

    def source(k, j):
        weight = stiff_ref[k] * blend_of(depth, mine, cells, k)
        return [pivot_ref[k, 3 * a + j] * weight for a in range(3)]

    for j in range(3):
        column = [pivot_ref[0, 3 * a + j] * first for a in range(3)]
        forced = source(0, j)
        for a in range(3):
            prefix[0, a] = column[a]
            driven[0, a] = forced[a]
        for k in range(1, cells):
            here = link(k)
            column = product(pivot_ref, k, [here * v for v in column])
            added = source(k, j)
            forced = product(pivot_ref, k, [here * v for v in forced])
            forced = [forced[a] + added[a] for a in range(3)]
            for a in range(3):
                prefix[k, a] = column[a]
                driven[k, a] = forced[a]
        for a in range(3):
            put_lines(out_ref, 3 * a + j, MAP_ROWS, column[a])
            put_lines(out_ref, 27 + 3 * a + j, MAP_ROWS, forced[a])
        upper = [pivot_ref[cells - 1, 3 * a + j] for a in range(3)]
        for k in range(cells - 2, -1, -1):
            above = link(k + 1)
            column = product(pivot_ref, k, [above * v for v in column])
            column = [column[a] + prefix[k, a] for a in range(3)]
            forced = product(pivot_ref, k, [above * v for v in forced])
            forced = [forced[a] + driven[k, a] for a in range(3)]
            upper = product(pivot_ref, k, [above * v for v in upper])
        for a in range(3):
            put_lines(out_ref, 9 + 3 * a + j, MAP_ROWS, first * upper[a])
            put_lines(out_ref, 18 + 3 * a + j, MAP_ROWS, first * column[a])
            put_lines(out_ref, 36 + 3 * a + j, MAP_ROWS, first * forced[a])
    blank = jnp.zeros_like(first)
    for a in range(45, MAP_ROWS):
        put_lines(out_ref, a, MAP_ROWS, blank)


def wall_kernel(mine, *rest):
    far, (keep_ref, send_ref, mask_ref), near = rest[:5], rest[5:8], rest[8:13]
    sums, blocks, arrived = rest[13:]
    copies = [pltpu.make_async_copy(far[i], near[i], arrived.at[i]) for i in range(5)]
    for copy in copies:
        copy.start()
    for copy in copies:
        copy.wait()
    mask_ref[...] = near[4][...]
    wall_parts(mine, *near, keep_ref, send_ref, sums, blocks)


def local_ends(pivot_ref, link, right_ref, values, out_ref):
    cells = pivot_ref.shape[0]
    for k in range(cells):
        state = [right_ref[k, b] for b in range(3)] if k == 0 else [
            right_ref[k, b] + link(k) * state[b] for b in range(3)
        ]
        state = product(pivot_ref, k, state)
        for b in range(3):
            values[k, b] = state[b]
    for b in range(3):
        put_lines(out_ref, b, END_ROWS, state[b])
    for k in range(cells - 2, -1, -1):
        above = link(k + 1)
        lifted = product(pivot_ref, k, [above * v for v in state])
        state = [values[k, b] + lifted[b] for b in range(3)]
    first = link(0)
    for b in range(3):
        put_lines(out_ref, 3 + b, END_ROWS, first * state[b])
    blank = jnp.zeros_like(first)
    for b in range(6, END_ROWS):
        put_lines(out_ref, b, END_ROWS, blank)


def around(value, low, high):
    rows = lax.broadcasted_iota(jnp.int32, value.shape, 0)
    columns = lax.broadcasted_iota(jnp.int32, value.shape, 1)
    height, width = value.shape
    below = jnp.where(rows == 0, low, pltpu.roll(value, 1, 0))
    above = jnp.where(rows == height - 1, high, pltpu.roll(value, height - 1, 0))
    left = jnp.where(columns == 0, 0.0, pltpu.roll(value, 1, 1))
    right = jnp.where(columns == width - 1, 0.0, pltpu.roll(value, width - 1, 1))
    return (below + above) + (left + right)


def next_kernel(mine, shape_ref, outer_ref, inner_ref, pivot_ref, coupling_ref, offsets_ref,
                stiff_ref, right_ref, out_ref, values, low_rows, high_rows):
    cells = pivot_ref.shape[0]
    even = lax.rem(mine[0], 2) == 0
    inner, outer = inner_ref[...].astype(F32), outer_ref[...].astype(F32)
    low_rows[...] = jnp.where(even, outer, inner)
    high_rows[...] = jnp.where(even, inner, outer)
    for k in range(cells):
        for c in range(3):
            row = 3 * k + c
            summed = around(
                shape_ref[k, c], low_rows[row : row + 1, :], high_rows[row : row + 1, :]
            )
            right_ref[k, c] = stiff_ref[k] * summed
    link = links_of(mine, coupling_ref, offsets_ref)
    local_ends(pivot_ref, link, right_ref, values, out_ref)


def row_of(ref, row):
    return ref[row : row + 1, :]


def apply_map(maps_ref, base, vector):
    return [
        row_of(maps_ref, base + 3 * a) * vector[0]
        + row_of(maps_ref, base + 3 * a + 1) * vector[1]
        + row_of(maps_ref, base + 3 * a + 2) * vector[2]
        for a in range(3)
    ]


def chain(maps_ref, ends, wall, out_ref, stride):
    places = maps_ref.shape[0] // MAP_ROWS
    state = wall
    tops = []
    for place in range(places):
        base = place * MAP_ROWS
        end, top = ends(place)
        for c in range(3):
            out_ref[place * stride + c : place * stride + c + 1, :] = state[c]
        reflected = apply_map(maps_ref, base + 18, state)
        tops.append([top[c] + reflected[c] for c in range(3)])
        moved = apply_map(maps_ref, base, state)
        state = [end[c] + moved[c] for c in range(3)]
    state = [jnp.zeros((1, LANES), F32)] * 3
    for place in range(places - 1, -1, -1):
        for c in range(3):
            out_ref[place * stride + 3 + c : place * stride + 4 + c, :] = state[c]
        moved = apply_map(maps_ref, place * MAP_ROWS + 9, state)
        state = [tops[place][c] + moved[c] for c in range(3)]


def first_chain_kernel(mine, maps_ref, mask_ref, keep_ref, got_ref, out_ref, wall_ref, sums, masks):
    places = maps_ref.shape[0] // MAP_ROWS
    row, half = owned(mine)
    sums[...] = keep_ref[...] + got_ref[...]
    mask = mask_ref[...].astype(F32)
    masks[0, 8:16, :] = mask[:, :LANES]
    masks[1, 8:16, :] = mask[:, LANES:]
    masks[half, 7:8, :] = row_of(sums, 12)
    masks[half, 16:17, :] = row_of(sums, 13)
    low_mask = masks[half, pl.ds(7 + row, 1), :]
    own_mask = masks[half, pl.ds(8 + row, 1), :]
    high_mask = masks[half, pl.ds(9 + row, 1), :]
    other_mask = masks[1 - half, pl.ds(8 + row, 1), :]
    lane = lax.broadcasted_iota(jnp.int32, (1, LANES), 1)
    wall, around_wall = [], []
    for c in range(3):
        own = row_of(sums, 3 + c) * own_mask
        other = row_of(sums, 9 + c) * other_mask
        left_edge = jnp.where(half == 1, pltpu.roll(other, 1, 1), 0.0)
        right_edge = jnp.where(half == 0, pltpu.roll(other, LANES - 1, 1), 0.0)
        left = jnp.where(lane == 0, left_edge, pltpu.roll(own, 1, 1))
        right = jnp.where(lane == LANES - 1, right_edge, pltpu.roll(own, LANES - 1, 1))
        ends = row_of(sums, c) * low_mask + row_of(sums, 6 + c) * high_mask
        wall.append(own)
        around_wall.append(ends + (left + right))
        wall_ref[c : c + 1, :] = own

    def ends_at(place):
        base = place * MAP_ROWS
        return (
            apply_map(maps_ref, base + 27, around_wall),
            apply_map(maps_ref, base + 36, around_wall),
        )

    chain(maps_ref, ends_at, wall, out_ref, FLOW_ROWS)
    for place in range(places):
        base = place * FLOW_ROWS
        for c in range(3):
            out_ref[base + 6 + c : base + 7 + c, :] = around_wall[c]


def next_chain_kernel(mine, maps_ref, ends_ref, wall_ref, out_ref):
    def ends_at(place):
        base = place * END_ROWS
        return (
            [row_of(ends_ref, base + c) for c in range(3)],
            [row_of(ends_ref, base + 3 + c) for c in range(3)],
        )

    chain(maps_ref, ends_at, [row_of(wall_ref, c) for c in range(3)], out_ref, END_ROWS)
    for place in range(ends_ref.shape[0] // END_ROWS):
        base = place * END_ROWS
        out_ref[base + 6 : base + 8, :] = jnp.zeros((2, LANES), F32)


def solve(mine, flows_ref, stride, right, pivot_ref, coupling_ref, offsets_ref, shape_ref, edges, values):
    cells = pivot_ref.shape[0]
    width = shape_ref.shape[3]
    link = links_of(mine, coupling_ref, offsets_ref)
    state = [get_lines(flows_ref, c, stride, width) for c in range(3)]
    for k in range(cells):
        here = link(k)
        given = right(k)
        state = product(pivot_ref, k, [given[b] + here * state[b] for b in range(3)])
        for b in range(3):
            values[k, b] = state[b]
    lifted = [get_lines(flows_ref, 3 + c, stride, width) for c in range(3)]
    for k in range(cells - 1, -1, -1):
        lifted = product(pivot_ref, k, lifted)
        state = [values[k, b] + lifted[b] for b in range(3)]
        for b in range(3):
            shape_ref[k, b] = state[b]
            if edges:
                row = 3 * k + b
                edges[2][row : row + 1, :] = state[b][0:1]
                edges[3][row : row + 1, :] = state[b][7:8]
        if k:
            here = link(k)
            lifted = [here * v for v in state]
    if edges:
        even = lax.rem(mine[0], 2) == 0
        first, final = edges[2][...], edges[3][...]
        edges[0][...] = jnp.where(even, final, first).astype(jnp.bfloat16)
        edges[1][...] = jnp.where(even, first, final).astype(jnp.bfloat16)


def first_solve_kernel(depth, mine, flows_ref, stiff_ref, pivot_ref, coupling_ref, offsets_ref,
                       shape_ref, inner_ref, outer_ref, values, first_rows, last_rows):
    cells = pivot_ref.shape[0]
    width = shape_ref.shape[3]
    around_wall = [get_lines(flows_ref, 6 + c, FLOW_ROWS, width) for c in range(3)]

    def right(k):
        weight = stiff_ref[k] * blend_of(depth, mine, cells, k)
        return [weight * v for v in around_wall]

    edges = (inner_ref, outer_ref, first_rows, last_rows)
    solve(mine, flows_ref, FLOW_ROWS, right, pivot_ref, coupling_ref, offsets_ref, shape_ref, edges, values)


def solve_kernel(mine, flows_ref, right_ref, pivot_ref, coupling_ref, offsets_ref, shape_ref, *rest):
    def right(k):
        return [right_ref[k, b] for b in range(3)]

    edges = (rest[0], rest[1], rest[3], rest[4]) if len(rest) > 1 else ()
    values = rest[2] if edges else rest[0]
    solve(mine, flows_ref, END_ROWS, right, pivot_ref, coupling_ref, offsets_ref, shape_ref, edges, values)


def per_device(
    mode_shapes,
    amplitude,
    mode_patch,
    column_patch,
    wall_mask,
    offsets,
    coupling,
    pivot_inv,
    stiffness,
):
    rows, width = wall_mask.shape
    cells = coupling.shape[0]
    surf, norm = lax.axis_size("surf"), lax.axis_size("norm")
    modes = jnp.transpose(mode_shapes, (0, 2, 1, 3))
    pivots = jnp.transpose(pivot_inv, (0, 2, 1, 3))
    cube = shaped(cells, 3, rows, width)
    scratch = pltpu.VMEM((cells, 3, rows, width), F32)
    edge = shaped(cells * 3, width, dtype=jnp.bfloat16)
    edge_scratch = pltpu.VMEM((cells * 3, width), F32)
    depth = cells * norm

    def swapped(block, axis, count):
        block = block.reshape((count, block.shape[0] // count) + block.shape[1:])
        block = lax.all_to_all(block, axis, 0, 0, tiled=True)
        return block.reshape((-1,) + block.shape[2:])

    def paired(part, bits):
        return lax.ppermute(part, "surf", [(i, i ^ bits) for i in range(surf)])

    size = surf * WALL_ROWS // 2
    given = (amplitude, mode_patch, modes, column_patch, wall_mask)
    keep, send, mask = call(
        wall_kernel,
        [shaped(size, LANES), shaped(size, LANES), shaped(rows, width, dtype=wall_mask.dtype)],
        [(pltpu.SMEM if a.ndim == 1 else pltpu.VMEM)(a.shape, a.dtype) for a in given]
        + [
            pltpu.VMEM((6, mode_shapes.shape[1] + 16, LANES), F32),
            pltpu.VMEM((2 * size, LANES), F32),
            pltpu.SemaphoreType.DMA((5,)),
        ],
        given,
        "walls",
        far=True,
    )
    got = paired(send, 1)
    (maps,) = call(
        functools.partial(maps_kernel, depth),
        [shaped(norm * MAP_ROWS, LANES)],
        [scratch, scratch],
        (pivots, coupling, offsets, stiffness),
        "maps",
    )
    maps, got = lax.optimization_barrier((maps, got))
    for shift in (3, 1):
        size //= 2
        keep, send = call(
            functools.partial(wall_sum_kernel, shift),
            [shaped(size, LANES)] * 2,
            [pltpu.VMEM((2 * size, LANES), F32)],
            (keep, got),
            "wall_sum",
        )
        got = paired(send, 1 << shift)
        if shift == 3:
            maps = swapped(maps, "norm", norm)
        size //= 2
        keep, send = call(wall_half_kernel, [shaped(size, LANES)] * 2, [], (keep, got), "wall_half")
        got = paired(send, 3 << shift)
    flows, wall = call(
        first_chain_kernel,
        [shaped(norm * FLOW_ROWS, LANES), shaped(8, LANES)],
        [pltpu.VMEM((WALL_ROWS, LANES), F32), pltpu.VMEM((2, 24, LANES), F32)],
        (maps, mask, keep, got),
        "first_chain",
    )
    flows = swapped(flows, "norm", norm)
    local = (pivots, coupling, offsets)
    edges = [scratch, edge_scratch, edge_scratch]
    shape, inner, outer = call(
        functools.partial(first_solve_kernel, depth),
        [cube, edge, edge],
        edges,
        (flows, stiffness) + local,
        "first_solve",
    )
    for sweep in range(1, SWEEPS):
        outer = lax.ppermute(
            outer, "surf", [(i, (i - 1 + 2 * (i % 2)) % surf) for i in range(surf)]
        )
        inner = lax.ppermute(inner, "surf", [(i, i + 1 - 2 * (i % 2)) for i in range(surf)])
        right, ends = call(
            next_kernel,
            [cube, shaped(norm * END_ROWS, LANES)],
            edges,
                (shape, outer, inner) + local + (stiffness,),
            "next_ends",
        )
        ends = swapped(ends, "norm", norm)
        (flows,) = call(
            next_chain_kernel, [shaped(norm * END_ROWS, LANES)], [], (maps, ends, wall), "chain"
        )
        flows = swapped(flows, "norm", norm)
        last = sweep == SWEEPS - 1
        solved = call(
            solve_kernel,
            [cube] if last else [cube, edge, edge],
            [scratch] if last else edges,
                (flows, right) + local,
            "solve",
        )
        if not last:
            shape, inner, outer = solved
    return jnp.transpose(solved[0], (0, 2, 1, 3))


def solution(mesh):
    return jax.shard_map(
        per_device,
        mesh=mesh,
        in_specs=(
            P("surf", None, None, None),
            P(),
            P(),
            P(),
            P("surf", None),
            P("surf", None),
            P("norm", "surf", None),
            P("norm", "surf", None, None),
            P("norm", "surf", None),
        ),
        out_specs=P("norm", "surf", None, None),
        check_vma=False,
    )
```

```python
import functools
import jax
import jax.numpy as jnp
from jax import lax
from jax.experimental import pallas as pl
from jax.experimental.pallas import tpu as pltpu
from jax.sharding import PartitionSpec as P

SWEEPS = 3
F32 = jnp.float32
LANES = 128
MAP_ROWS = 48
WALL_ROWS = 16
MAP_STEP = 56
WALL_STEP = 24
FLOW_ROWS = 16
END_ROWS = 8
VMEM_LIMIT = 16 * 1024 * 1024
VMEM_FRONT = 60 * 1024 * 1024


def call(kernel, outs, scratch, args, name, far=False, out_far=False):
    space = pltpu.HBM if far else pltpu.VMEM
    moved = sum(a.size * a.dtype.itemsize for a in list(args) + list(outs))

    def body(*refs):
        kernel((lax.axis_index("surf"), lax.axis_index("norm")), *refs)

    return pl.pallas_call(
        body,
        out_shape=outs,
        in_specs=[pl.BlockSpec(memory_space=space) for _ in args],
        out_specs=[pl.BlockSpec(memory_space=pltpu.HBM if out_far else pltpu.VMEM) for _ in outs],
        scratch_shapes=scratch,
        name=name,
        cost_estimate=pl.CostEstimate(flops=1000000, bytes_accessed=moved, transcendentals=0),
        compiler_params=pltpu.CompilerParams(vmem_limit_bytes=VMEM_FRONT if far else VMEM_LIMIT),
    )(*args)


def shaped(*shape, dtype=F32):
    return jax.ShapeDtypeStruct(shape, dtype)


def wall_parts(arrive, mine, amplitude_ref, patch_ref, modes_ref, columns_ref, mask_ref, keep_ref, send_ref, sums, blocks):
    own_modes = modes_ref.shape[0]
    count = modes_ref.shape[2]
    parts = blocks.shape[0] // WALL_STEP
    base = mine[0] * own_modes
    row, half = owned(mine)

    def one(block, carry):
        rows = pl.ds(pl.multiple_of(block * 16, 16), 16)
        target = pl.ds(pl.multiple_of(block * 16 + 8, 8), 16)
        patch = columns_ref[rows, :]
        weights = [
            jnp.where(patch == patch_ref[base + m], amplitude_ref[base + m], 0.0)
            for m in range(own_modes)
        ]
        for c in range(3):
            total = weights[0] * modes_ref[0, c, rows, :].astype(F32)
            for m in range(1, own_modes):
                total = total + weights[m] * modes_ref[m, c, rows, :].astype(F32)
            sums[2 * c, target, :] = total[:, :LANES]
            sums[2 * c + 1, target, :] = total[:, LANES:]
        return carry

    for piece in range(count // 64):
        arrive(piece)
        lax.fori_loop(4 * piece, 4 * piece + 4, one, 0)
    for c in range(6):
        sums[c, 0:8, :] = sums[c, count : count + 8, :]
        sums[c, count + 8 : count + 16, :] = sums[c, 8:16, :]

    def put(place, from_ref, start):
        for odd in range(2):
            blocks[pl.ds(odd * (parts // 2) * WALL_STEP + place, parts // 2, stride=WALL_STEP), :] = (
                from_ref[pl.ds(start + 8 * odd, parts // 2, stride=16), :]
            )

    for c in range(3):
        for step in range(3):
            put(3 * step + c, sums.at[2 * c + half], 7 + row + step)
        put(9 + c, sums.at[2 * c + 1 - half], 8 + row)
    blank = jnp.zeros((parts, LANES), F32)
    for place in range(12, 16):
        blocks[pl.ds(place, parts, stride=WALL_STEP), :] = blank
    mask = jnp.where(half == 0, mask_ref[:, :LANES], mask_ref[:, LANES:]).astype(F32)
    for step, place, edge in ((1, 12, 7), (parts - 1, 13, 0)):
        target = lax.rem(mine[0] + step, parts)
        order = lax.rem(target, 2) * (parts // 2) + lax.div(target, 2)
        blocks[pl.ds(order * WALL_STEP + place, 1), :] = mask[edge : edge + 1]
    side = lax.rem(mine[0], 2)
    for ref, first in ((keep_ref, side), (send_ref, 1 - side)):
        for i in range(parts // 2):
            start = pl.multiple_of((first * (parts // 2) + i) * WALL_STEP, 8)
            ref[i * WALL_ROWS : (i + 1) * WALL_ROWS, :] = blocks[pl.ds(start, WALL_ROWS), :]


def wall_sum_kernel(shift, mine, keep_ref, got_ref, next_ref, send_ref, blocks):
    blocks[...] = keep_ref[...] + got_ref[...]
    rows = keep_ref.shape[0] // 4
    own = lax.rem(lax.shift_right_logical(mine[0], shift), 4)
    for ref, steps in ((next_ref, (0, 3)), (send_ref, (1, 2))):
        for i, step in enumerate(steps):
            start = pl.multiple_of(lax.bitwise_xor(own, step) * rows, 16)
            ref[i * rows : (i + 1) * rows, :] = blocks[pl.ds(start, rows), :]


def wall_half_kernel(mine, keep_ref, got_ref, next_ref, send_ref):
    rows = next_ref.shape[0]
    next_ref[...] = keep_ref[:rows] + got_ref[:rows]
    send_ref[...] = keep_ref[rows:] + got_ref[rows:]


def owned(mine):
    return lax.rem(mine[1], 8), lax.div(mine[1], 8)


def links_of(mine, coupling_ref, offsets_ref):
    cells = coupling_ref.shape[0]
    cut = offsets_ref[...] - mine[1] * cells

    def link(k):
        return jnp.where(cut == k, 0.0, coupling_ref[k])

    return link


def product(pivot_ref, k, vector):
    return [
        pivot_ref[k, 3 * a] * vector[0]
        + pivot_ref[k, 3 * a + 1] * vector[1]
        + pivot_ref[k, 3 * a + 2] * vector[2]
        for a in range(3)
    ]


def put_lines(out_ref, row, stride, value):
    for half in range(value.shape[1] // LANES):
        out_ref[pl.ds(half * 8 * stride + row, 8, stride=stride), :] = value[
            :, half * LANES : (half + 1) * LANES
        ]


def get_lines(in_ref, row, stride, width):
    return jnp.concatenate(
        [
            in_ref[pl.ds(half * 8 * stride + row, 8, stride=stride), :]
            for half in range(width // LANES)
        ],
        axis=1,
    )


def blend_of(depth, mine, cells, k):
    return 1.0 - (mine[1] * cells + k).astype(F32) * (1.0 / depth)


def maps_kernel(depth, mine, pivot_ref, coupling_ref, offsets_ref, stiff_ref, out_ref, prefix, driven, spread):
    cells = pivot_ref.shape[0]
    link = links_of(mine, coupling_ref, offsets_ref)
    first = link(0)

    def source(k, j):
        weight = stiff_ref[k] * blend_of(depth, mine, cells, k)
        return [pivot_ref[k, 3 * a + j] * weight for a in range(3)]

    for j in range(3):
        column = [pivot_ref[0, 3 * a + j] * first for a in range(3)]
        forced = source(0, j)
        for a in range(3):
            prefix[0, a] = column[a]
            driven[0, a] = forced[a]
        for k in range(1, cells):
            here = link(k)
            column = product(pivot_ref, k, [here * v for v in column])
            added = source(k, j)
            forced = product(pivot_ref, k, [here * v for v in forced])
            forced = [forced[a] + added[a] for a in range(3)]
            for a in range(3):
                prefix[k, a] = column[a]
                driven[k, a] = forced[a]
        for a in range(3):
            put_lines(spread, 3 * a + j, MAP_STEP, column[a])
            put_lines(spread, 27 + 3 * a + j, MAP_STEP, forced[a])
        upper = [pivot_ref[cells - 1, 3 * a + j] for a in range(3)]
        for k in range(cells - 2, -1, -1):
            above = link(k + 1)
            column = product(pivot_ref, k, [above * v for v in column])
            column = [column[a] + prefix[k, a] for a in range(3)]
            forced = product(pivot_ref, k, [above * v for v in forced])
            forced = [forced[a] + driven[k, a] for a in range(3)]
            upper = product(pivot_ref, k, [above * v for v in upper])
        for a in range(3):
            put_lines(spread, 9 + 3 * a + j, MAP_STEP, first * upper[a])
            put_lines(spread, 18 + 3 * a + j, MAP_STEP, first * column[a])
            put_lines(spread, 36 + 3 * a + j, MAP_STEP, first * forced[a])
    blank = jnp.zeros_like(first)
    for a in range(45, MAP_ROWS):
        put_lines(spread, a, MAP_STEP, blank)
    for place in range(out_ref.shape[0] // MAP_ROWS):
        out_ref[place * MAP_ROWS : (place + 1) * MAP_ROWS, :] = spread[
            place * MAP_STEP : place * MAP_STEP + MAP_ROWS, :
        ]


def wall_kernel(mine, *rest):
    far, (keep_ref, send_ref, mask_ref), near = rest[:5], rest[5:8], rest[8:13]
    sums, blocks, arrived, pieces = rest[13:]
    modes = [
        pltpu.make_async_copy(
            far[2].at[:, :, 64 * i : 64 * (i + 1), :],
            near[2].at[:, :, 64 * i : 64 * (i + 1), :],
            pieces.at[i],
        )
        for i in range(near[2].shape[2] // 64)
    ]
    whole = [pltpu.make_async_copy(far[i], near[i], arrived.at[i]) for i in (0, 1, 3, 4)]
    for copy in whole + modes:
        copy.start()
    for copy in whole:
        copy.wait()
    mask_ref[...] = near[4][...]
    wall_parts(lambda i: modes[i].wait(), mine, *near, keep_ref, send_ref, sums, blocks)


def local_ends(pivot_ref, link, right_ref, values, out_ref):
    cells = pivot_ref.shape[0]
    for k in range(cells):
        state = [right_ref[k, b] for b in range(3)] if k == 0 else [
            right_ref[k, b] + link(k) * state[b] for b in range(3)
        ]
        state = product(pivot_ref, k, state)
        for b in range(3):
            values[k, b] = state[b]
    for b in range(3):
        put_lines(out_ref, b, END_ROWS, state[b])
    for k in range(cells - 2, -1, -1):
        above = link(k + 1)
        lifted = product(pivot_ref, k, [above * v for v in state])
        state = [values[k, b] + lifted[b] for b in range(3)]
    first = link(0)
    for b in range(3):
        put_lines(out_ref, 3 + b, END_ROWS, first * state[b])
    blank = jnp.zeros_like(first)
    for b in range(6, END_ROWS):
        put_lines(out_ref, b, END_ROWS, blank)


def around(value, low, high):
    rows = lax.broadcasted_iota(jnp.int32, value.shape, 0)
    columns = lax.broadcasted_iota(jnp.int32, value.shape, 1)
    height, width = value.shape
    below = jnp.where(rows == 0, low, pltpu.roll(value, 1, 0))
    above = jnp.where(rows == height - 1, high, pltpu.roll(value, height - 1, 0))
    left = jnp.where(columns == 0, 0.0, pltpu.roll(value, 1, 1))
    right = jnp.where(columns == width - 1, 0.0, pltpu.roll(value, width - 1, 1))
    return (below + above) + (left + right)


def next_kernel(mine, shape_ref, outer_ref, inner_ref, pivot_ref, coupling_ref, offsets_ref,
                stiff_ref, right_ref, out_ref, values, low_rows, high_rows):
    cells = pivot_ref.shape[0]
    even = lax.rem(mine[0], 2) == 0
    inner, outer = inner_ref[...].astype(F32), outer_ref[...].astype(F32)
    low_rows[...] = jnp.where(even, outer, inner)
    high_rows[...] = jnp.where(even, inner, outer)
    for k in range(cells):
        for c in range(3):
            row = 3 * k + c
            summed = around(
                shape_ref[k, c], low_rows[row : row + 1, :], high_rows[row : row + 1, :]
            )
            right_ref[k, c] = stiff_ref[k] * summed
    link = links_of(mine, coupling_ref, offsets_ref)
    local_ends(pivot_ref, link, right_ref, values, out_ref)


def row_of(ref, row):
    return ref[row : row + 1, :]


def apply_map(maps_ref, base, vector):
    return [
        row_of(maps_ref, base + 3 * a) * vector[0]
        + row_of(maps_ref, base + 3 * a + 1) * vector[1]
        + row_of(maps_ref, base + 3 * a + 2) * vector[2]
        for a in range(3)
    ]


def chain(maps_ref, ends, wall, put):
    places = maps_ref.shape[0] // MAP_ROWS
    state = wall
    tops = []
    for place in range(places):
        base = place * MAP_ROWS
        end, top = ends(place)
        for c in range(3):
            put(place, c, state[c])
        reflected = apply_map(maps_ref, base + 18, state)
        tops.append([top[c] + reflected[c] for c in range(3)])
        moved = apply_map(maps_ref, base, state)
        state = [end[c] + moved[c] for c in range(3)]
    state = [jnp.zeros((1, LANES), F32)] * 3
    for place in range(places - 1, -1, -1):
        for c in range(3):
            put(place, 3 + c, state[c])
        moved = apply_map(maps_ref, place * MAP_ROWS + 9, state)
        state = [tops[place][c] + moved[c] for c in range(3)]


def first_chain_kernel(mine, maps_ref, mask_ref, keep_ref, got_ref, out_ref, wall_ref, sums, masks, flows):
    places = maps_ref.shape[0] // MAP_ROWS
    row, half = owned(mine)
    sums[...] = keep_ref[...] + got_ref[...]
    mask = mask_ref[...].astype(F32)
    masks[0, 8:16, :] = mask[:, :LANES]
    masks[1, 8:16, :] = mask[:, LANES:]
    masks[half, 7:8, :] = row_of(sums, 12)
    masks[half, 16:17, :] = row_of(sums, 13)
    low_mask = masks[half, pl.ds(7 + row, 1), :]
    own_mask = masks[half, pl.ds(8 + row, 1), :]
    high_mask = masks[half, pl.ds(9 + row, 1), :]
    other_mask = masks[1 - half, pl.ds(8 + row, 1), :]
    lane = lax.broadcasted_iota(jnp.int32, (1, LANES), 1)
    wall, around_wall = [], []
    for c in range(3):
        own = row_of(sums, 3 + c) * own_mask
        other = row_of(sums, 9 + c) * other_mask
        left_edge = jnp.where(half == 1, pltpu.roll(other, 1, 1), 0.0)
        right_edge = jnp.where(half == 0, pltpu.roll(other, LANES - 1, 1), 0.0)
        left = jnp.where(lane == 0, left_edge, pltpu.roll(own, 1, 1))
        right = jnp.where(lane == LANES - 1, right_edge, pltpu.roll(own, LANES - 1, 1))
        ends = row_of(sums, c) * low_mask + row_of(sums, 6 + c) * high_mask
        wall.append(own)
        around_wall.append(ends + (left + right))
        wall_ref[c : c + 1, :] = own

    def ends_at(place):
        base = place * MAP_ROWS
        return (
            apply_map(maps_ref, base + 27, around_wall),
            apply_map(maps_ref, base + 36, around_wall),
        )

    def put(place, c, value):
        row = place * FLOW_ROWS + 2 * c
        rounded = value.astype(jnp.bfloat16).astype(F32)
        flows[row : row + 1, :] = rounded
        flows[row + 1 : row + 2, :] = value - rounded

    chain(maps_ref, ends_at, wall, put)
    for place in range(places):
        row = place * FLOW_ROWS + 12
        for c in range(3):
            flows[row + c : row + c + 1, :] = around_wall[c]
        flows[row + 3 : row + 4, :] = jnp.zeros((1, LANES), F32)
    out_ref[...] = flows[...].astype(jnp.bfloat16)


def next_chain_kernel(mine, maps_ref, ends_ref, wall_ref, out_ref):
    def ends_at(place):
        base = place * END_ROWS
        return (
            [row_of(ends_ref, base + c) for c in range(3)],
            [row_of(ends_ref, base + 3 + c) for c in range(3)],
        )

    def put(place, c, value):
        out_ref[place * END_ROWS + c : place * END_ROWS + c + 1, :] = value

    chain(maps_ref, ends_at, [row_of(wall_ref, c) for c in range(3)], put)
    for place in range(ends_ref.shape[0] // END_ROWS):
        base = place * END_ROWS
        out_ref[base + 6 : base + 8, :] = jnp.zeros((2, LANES), F32)


def solve(mine, flow, right, pivot_ref, coupling_ref, offsets_ref, shape_ref, edges, values, done=None):
    cells = pivot_ref.shape[0]
    link = links_of(mine, coupling_ref, offsets_ref)
    state = [flow(c) for c in range(3)]
    for k in range(cells):
        here = link(k)
        given = right(k)
        state = product(pivot_ref, k, [given[b] + here * state[b] for b in range(3)])
        for b in range(3):
            values[k, b] = state[b]
    lifted = [flow(3 + c) for c in range(3)]
    for k in range(cells - 1, -1, -1):
        lifted = product(pivot_ref, k, lifted)
        state = [values[k, b] + lifted[b] for b in range(3)]
        for b in range(3):
            shape_ref[k, b] = state[b]
            if edges:
                row = 3 * k + b
                edges[2][row : row + 1, :] = state[b][0:1]
                edges[3][row : row + 1, :] = state[b][7:8]
        if done:
            done(k)
        if k:
            here = link(k)
            lifted = [here * v for v in state]
    if edges:
        even = lax.rem(mine[0], 2) == 0
        first, final = edges[2][...], edges[3][...]
        edges[0][...] = jnp.where(even, final, first).astype(jnp.bfloat16)
        edges[1][...] = jnp.where(even, first, final).astype(jnp.bfloat16)


def first_solve_kernel(depth, mine, flows_ref, stiff_ref, pivot_ref, coupling_ref, offsets_ref,
                       shape_ref, inner_ref, outer_ref, values, first_rows, last_rows, flows):
    cells = pivot_ref.shape[0]
    width = shape_ref.shape[3]
    flows[...] = flows_ref[...].astype(F32)
    around_wall = [get_lines(flows, 12 + c, FLOW_ROWS, width) for c in range(3)]

    def flow(c):
        return get_lines(flows, 2 * c, FLOW_ROWS, width) + get_lines(flows, 2 * c + 1, FLOW_ROWS, width)

    def right(k):
        weight = stiff_ref[k] * blend_of(depth, mine, cells, k)
        return [weight * v for v in around_wall]

    edges = (inner_ref, outer_ref, first_rows, last_rows)
    solve(mine, flow, right, pivot_ref, coupling_ref, offsets_ref, shape_ref, edges, values)


def solve_kernel(mine, flows_ref, right_ref, pivot_ref, coupling_ref, offsets_ref, shape_ref, *rest):
    def right(k):
        return [right_ref[k, b] for b in range(3)]

    def flow(c):
        return get_lines(flows_ref, c, END_ROWS, shape_ref.shape[3])

    local = (pivot_ref, coupling_ref, offsets_ref)
    if len(rest) > 3:
        edges = (rest[0], rest[1], rest[3], rest[4])
        solve(mine, flow, right, *local, shape_ref, edges, rest[2])
        return
    values, near, sent = rest
    pieces = [
        pltpu.make_async_copy(near.at[4 * i : 4 * i + 4], shape_ref.at[4 * i : 4 * i + 4], sent.at[i])
        for i in range(near.shape[0] // 4)
    ]

    def done(k):
        if k % 4 == 0:
            pieces[k // 4].start()

    solve(mine, flow, right, *local, near, (), values, done)
    for piece in pieces:
        piece.wait()


def per_device(
    mode_shapes,
    amplitude,
    mode_patch,
    column_patch,
    wall_mask,
    offsets,
    coupling,
    pivot_inv,
    stiffness,
):
    rows, width = wall_mask.shape
    cells = coupling.shape[0]
    surf, norm = lax.axis_size("surf"), lax.axis_size("norm")
    modes = jnp.transpose(mode_shapes, (0, 2, 1, 3))
    pivots = jnp.transpose(pivot_inv, (0, 2, 1, 3))
    cube = shaped(cells, 3, rows, width)
    scratch = pltpu.VMEM((cells, 3, rows, width), F32)
    edge = shaped(cells * 3, width, dtype=jnp.bfloat16)
    edge_scratch = pltpu.VMEM((cells * 3, width), F32)
    depth = cells * norm

    def swapped(block, axis, count):
        block = block.reshape((count, block.shape[0] // count) + block.shape[1:])
        block = lax.all_to_all(block, axis, 0, 0, tiled=True)
        return block.reshape((-1,) + block.shape[2:])

    def paired(part, bits):
        return lax.ppermute(part, "surf", [(i, i ^ bits) for i in range(surf)])

    size = surf * WALL_ROWS // 2
    given = (amplitude, mode_patch, modes, column_patch, wall_mask)
    keep, send, mask = call(
        wall_kernel,
        [shaped(size, LANES), shaped(size, LANES), shaped(rows, width, dtype=wall_mask.dtype)],
        [(pltpu.SMEM if a.ndim == 1 else pltpu.VMEM)(a.shape, a.dtype) for a in given]
        + [
            pltpu.VMEM((6, mode_shapes.shape[1] + 16, LANES), F32),
            pltpu.VMEM((surf * WALL_STEP, LANES), F32),
            pltpu.SemaphoreType.DMA((5,)),
            pltpu.SemaphoreType.DMA((modes.shape[2] // 64,)),
        ],
        given,
        "walls",
        far=True,
    )
    got = paired(send, 1)
    (maps,) = call(
        functools.partial(maps_kernel, depth),
        [shaped(norm * MAP_ROWS, LANES)],
        [scratch, scratch, pltpu.VMEM((norm * MAP_STEP, LANES), F32)],
        (pivots, coupling, offsets, stiffness),
        "maps",
    )
    maps, got = lax.optimization_barrier((maps, got))
    for shift in (3, 1):
        size //= 2
        keep, send = call(
            functools.partial(wall_sum_kernel, shift),
            [shaped(size, LANES)] * 2,
            [pltpu.VMEM((2 * size, LANES), F32)],
            (keep, got),
            "wall_sum",
        )
        got = paired(send, 1 << shift)
        if shift == 3:
            maps = swapped(maps, "norm", norm)
        size //= 2
        keep, send = call(wall_half_kernel, [shaped(size, LANES)] * 2, [], (keep, got), "wall_half")
        got = paired(send, 3 << shift)
    flows, wall = call(
        first_chain_kernel,
        [shaped(norm * FLOW_ROWS, LANES, dtype=jnp.bfloat16), shaped(8, LANES)],
        [
            pltpu.VMEM((WALL_ROWS, LANES), F32),
            pltpu.VMEM((2, 24, LANES), F32),
            pltpu.VMEM((norm * FLOW_ROWS, LANES), F32),
        ],
        (maps, mask, keep, got),
        "first_chain",
    )
    flows = swapped(flows, "norm", norm)
    local = (pivots, coupling, offsets)
    edges = [scratch, edge_scratch, edge_scratch]
    shape, inner, outer = call(
        functools.partial(first_solve_kernel, depth),
        [cube, edge, edge],
        edges + [pltpu.VMEM((norm * FLOW_ROWS, LANES), F32)],
        (flows, stiffness) + local,
        "first_solve",
    )
    for sweep in range(1, SWEEPS):
        outer = lax.ppermute(
            outer, "surf", [(i, (i - 1 + 2 * (i % 2)) % surf) for i in range(surf)]
        )
        inner = lax.ppermute(inner, "surf", [(i, i + 1 - 2 * (i % 2)) for i in range(surf)])
        right, ends = call(
            next_kernel,
            [cube, shaped(norm * END_ROWS, LANES)],
            edges,
                (shape, outer, inner) + local + (stiffness,),
            "next_ends",
        )
        ends = swapped(ends, "norm", norm)
        (flows,) = call(
            next_chain_kernel, [shaped(norm * END_ROWS, LANES)], [], (maps, ends, wall), "chain"
        )
        flows = swapped(flows, "norm", norm)
        last = sweep == SWEEPS - 1
        solved = call(
            solve_kernel,
            [cube] if last else [cube, edge, edge],
            [scratch, scratch, pltpu.SemaphoreType.DMA((cells // 4,))] if last else edges,
                (flows, right) + local,
            "solve",
            out_far=last,
        )
        if not last:
            shape, inner, outer = solved
    return jnp.transpose(solved[0], (0, 2, 1, 3))


def solution(mesh):
    return jax.shard_map(
        per_device,
        mesh=mesh,
        in_specs=(
            P("surf", None, None, None),
            P(),
            P(),
            P(),
            P("surf", None),
            P("surf", None),
            P("norm", "surf", None),
            P("norm", "surf", None, None),
            P("norm", "surf", None),
        ),
        out_specs=P("norm", "surf", None, None),
        check_vma=False,
    )
```

```python
import functools
import jax
import jax.numpy as jnp
from jax import lax
from jax.experimental import pallas as pl
from jax.experimental.pallas import tpu as pltpu
from jax.sharding import PartitionSpec as P

SWEEPS = 3
F32 = jnp.float32
LANES = 128
MAP_ROWS = 48
WALL_ROWS = 16
MAP_STEP = 56
WALL_STEP = 24
FLOW_ROWS = 16
END_ROWS = 8
VMEM_LIMIT = 16 * 1024 * 1024
VMEM_FRONT = 60 * 1024 * 1024


def call(kernel, outs, scratch, args, name, far=False, out_far=False):
    space = pltpu.HBM if far else pltpu.VMEM
    moved = sum(a.size * a.dtype.itemsize for a in list(args) + list(outs))

    def body(*refs):
        kernel((lax.axis_index("surf"), lax.axis_index("norm")), *refs)

    return pl.pallas_call(
        body,
        out_shape=outs,
        in_specs=[pl.BlockSpec(memory_space=space) for _ in args],
        out_specs=[pl.BlockSpec(memory_space=pltpu.HBM if out_far else pltpu.VMEM) for _ in outs],
        scratch_shapes=scratch,
        name=name,
        cost_estimate=pl.CostEstimate(flops=1000000, bytes_accessed=moved, transcendentals=0),
        compiler_params=pltpu.CompilerParams(vmem_limit_bytes=VMEM_FRONT if far else VMEM_LIMIT),
    )(*args)


def shaped(*shape, dtype=F32):
    return jax.ShapeDtypeStruct(shape, dtype)


def wall_parts(arrive, mine, amplitude_ref, patch_ref, modes_ref, columns_ref, mask_ref, keep_ref, send_ref, sums, blocks):
    own_modes = modes_ref.shape[0]
    count = modes_ref.shape[2]
    parts = 2 * keep_ref.shape[0] // WALL_ROWS
    base = mine[0] * own_modes
    row, half = owned(mine)

    def one(block, carry):
        rows = pl.ds(pl.multiple_of(block * 16, 16), 16)
        target = pl.ds(pl.multiple_of(block * 16 + 8, 8), 16)
        patch = columns_ref[rows, :]
        weights = [
            jnp.where(patch == patch_ref[base + m], amplitude_ref[base + m], 0.0)
            for m in range(own_modes)
        ]
        for c in range(3):
            total = weights[0] * modes_ref[0, c, rows, :].astype(F32)
            for m in range(1, own_modes):
                total = total + weights[m] * modes_ref[m, c, rows, :].astype(F32)
            sums[2 * c, target, :] = total[:, :LANES]
            sums[2 * c + 1, target, :] = total[:, LANES:]
        return carry

    for piece in range(count // 64):
        arrive(piece)
        lax.fori_loop(4 * piece, 4 * piece + 4, one, 0)
    for c in range(6):
        sums[c, 0:8, :] = sums[c, count : count + 8, :]
        sums[c, count + 8 : count + 16, :] = sums[c, 8:16, :]

    def put(place, from_ref, start):
        for odd in range(2):
            blocks[pl.ds(odd * (parts // 2) * WALL_STEP + place, parts // 2, stride=WALL_STEP), :] = (
                from_ref[pl.ds(start + 8 * odd, parts // 2, stride=16), :]
            )

    for c in range(3):
        for step in range(3):
            put(3 * step + c, sums.at[2 * c + half], 7 + row + step)
        put(9 + c, sums.at[2 * c + 1 - half], 8 + row)
    blank = jnp.zeros((parts, LANES), F32)
    for place in range(12, 16):
        blocks[pl.ds(place, parts, stride=WALL_STEP), :] = blank
    mask = jnp.where(half == 0, mask_ref[:, :LANES], mask_ref[:, LANES:]).astype(F32)
    for step, place, edge in ((1, 12, 7), (parts - 1, 13, 0)):
        target = lax.rem(mine[0] + step, parts)
        order = lax.rem(target, 2) * (parts // 2) + lax.div(target, 2)
        blocks[pl.ds(order * WALL_STEP + place, 1), :] = mask[edge : edge + 1]
    side = lax.rem(mine[0], 2)
    for ref, first in ((keep_ref, side), (send_ref, 1 - side)):
        for i in range(parts // 2):
            start = pl.multiple_of((first * (parts // 2) + i) * WALL_STEP, 8)
            ref[i * WALL_ROWS : (i + 1) * WALL_ROWS, :] = blocks[pl.ds(start, WALL_ROWS), :]


def wall_sum_kernel(shift, mine, keep_ref, got_ref, next_ref, send_ref, blocks):
    blocks[...] = keep_ref[...] + got_ref[...]
    rows = keep_ref.shape[0] // 4
    own = lax.rem(lax.shift_right_logical(mine[0], shift), 4)
    for ref, steps in ((next_ref, (0, 3)), (send_ref, (1, 2))):
        for i, step in enumerate(steps):
            start = pl.multiple_of(lax.bitwise_xor(own, step) * rows, 16)
            ref[i * rows : (i + 1) * rows, :] = blocks[pl.ds(start, rows), :]


def wall_half_kernel(mine, keep_ref, got_ref, next_ref, send_ref):
    rows = next_ref.shape[0]
    next_ref[...] = keep_ref[:rows] + got_ref[:rows]
    send_ref[...] = keep_ref[rows:] + got_ref[rows:]


def owned(mine):
    return lax.rem(mine[1], 8), lax.div(mine[1], 8)


def links_of(mine, coupling_ref, offsets_ref):
    cells = coupling_ref.shape[0]
    cut = offsets_ref[...] - mine[1] * cells

    def link(k):
        return jnp.where(cut == k, 0.0, coupling_ref[k])

    return link


def product(pivot_ref, k, vector):
    return [
        pivot_ref[k, 3 * a] * vector[0]
        + pivot_ref[k, 3 * a + 1] * vector[1]
        + pivot_ref[k, 3 * a + 2] * vector[2]
        for a in range(3)
    ]


def put_lines(out_ref, row, stride, value):
    for half in range(value.shape[1] // LANES):
        out_ref[pl.ds(half * 8 * stride + row, 8, stride=stride), :] = value[
            :, half * LANES : (half + 1) * LANES
        ]


def get_lines(in_ref, row, stride, width):
    return jnp.concatenate(
        [
            in_ref[pl.ds(half * 8 * stride + row, 8, stride=stride), :]
            for half in range(width // LANES)
        ],
        axis=1,
    )


def blend_of(depth, mine, cells, k):
    return 1.0 - (mine[1] * cells + k).astype(F32) * (1.0 / depth)


def maps_kernel(depth, mine, pivot_ref, coupling_ref, offsets_ref, stiff_ref, out_ref, prefix, driven, spread):
    cells = pivot_ref.shape[0]
    link = links_of(mine, coupling_ref, offsets_ref)
    first = link(0)

    def source(k, j):
        weight = stiff_ref[k] * blend_of(depth, mine, cells, k)
        return [pivot_ref[k, 3 * a + j] * weight for a in range(3)]

    for j in range(3):
        column = [pivot_ref[0, 3 * a + j] * first for a in range(3)]
        forced = source(0, j)
        for a in range(3):
            prefix[0, a] = column[a]
            driven[0, a] = forced[a]
        for k in range(1, cells):
            here = link(k)
            column = product(pivot_ref, k, [here * v for v in column])
            added = source(k, j)
            forced = product(pivot_ref, k, [here * v for v in forced])
            forced = [forced[a] + added[a] for a in range(3)]
            for a in range(3):
                prefix[k, a] = column[a]
                driven[k, a] = forced[a]
        for a in range(3):
            put_lines(spread, 3 * a + j, MAP_STEP, column[a])
            put_lines(spread, 27 + 3 * a + j, MAP_STEP, forced[a])
        upper = [pivot_ref[cells - 1, 3 * a + j] for a in range(3)]
        for k in range(cells - 2, -1, -1):
            above = link(k + 1)
            column = product(pivot_ref, k, [above * v for v in column])
            column = [column[a] + prefix[k, a] for a in range(3)]
            forced = product(pivot_ref, k, [above * v for v in forced])
            forced = [forced[a] + driven[k, a] for a in range(3)]
            upper = product(pivot_ref, k, [above * v for v in upper])
        for a in range(3):
            put_lines(spread, 9 + 3 * a + j, MAP_STEP, first * upper[a])
            put_lines(spread, 18 + 3 * a + j, MAP_STEP, first * column[a])
            put_lines(spread, 36 + 3 * a + j, MAP_STEP, first * forced[a])
    blank = jnp.zeros_like(first)
    for a in range(45, MAP_ROWS):
        put_lines(spread, a, MAP_STEP, blank)
    for place in range(out_ref.shape[0] // MAP_ROWS):
        out_ref[place * MAP_ROWS : (place + 1) * MAP_ROWS, :] = spread[
            place * MAP_STEP : place * MAP_STEP + MAP_ROWS, :
        ]


def wall_kernel(mine, *rest):
    far, (keep_ref, send_ref, mask_ref), near = rest[:5], rest[5:8], rest[8:13]
    sums, blocks, arrived, pieces = rest[13:]
    modes = [
        pltpu.make_async_copy(
            far[2].at[:, :, 64 * i : 64 * (i + 1), :],
            near[2].at[:, :, 64 * i : 64 * (i + 1), :],
            pieces.at[i],
        )
        for i in range(near[2].shape[2] // 64)
    ]
    whole = [pltpu.make_async_copy(far[i], near[i], arrived.at[i]) for i in (0, 1, 3, 4)]
    for copy in whole + modes:
        copy.start()
    for copy in whole:
        copy.wait()
    mask_ref[...] = near[4][...]
    wall_parts(lambda i: modes[i].wait(), mine, *near, keep_ref, send_ref, sums, blocks)


def local_ends(pivot_ref, link, right_ref, values, spread, out_ref):
    cells = pivot_ref.shape[0]
    for k in range(cells):
        state = [right_ref[k, b] for b in range(3)] if k == 0 else [
            right_ref[k, b] + link(k) * state[b] for b in range(3)
        ]
        state = product(pivot_ref, k, state)
        for b in range(3):
            values[k, b] = state[b]
    for b in range(3):
        put_lines(spread, b, END_ROWS, state[b])
    for k in range(cells - 2, -1, -1):
        above = link(k + 1)
        lifted = product(pivot_ref, k, [above * v for v in state])
        state = [values[k, b] + lifted[b] for b in range(3)]
    first = link(0)
    for b in range(3):
        put_lines(spread, 3 + b, END_ROWS, first * state[b])
    blank = jnp.zeros_like(first)
    for b in range(6, END_ROWS):
        put_lines(spread, b, END_ROWS, blank)
    out_ref[...] = spread[: out_ref.shape[0], :]


def around(value, low, high):
    rows = lax.broadcasted_iota(jnp.int32, value.shape, 0)
    columns = lax.broadcasted_iota(jnp.int32, value.shape, 1)
    height, width = value.shape
    below = jnp.where(rows == 0, low, pltpu.roll(value, 1, 0))
    above = jnp.where(rows == height - 1, high, pltpu.roll(value, height - 1, 0))
    left = jnp.where(columns == 0, 0.0, pltpu.roll(value, 1, 1))
    right = jnp.where(columns == width - 1, 0.0, pltpu.roll(value, width - 1, 1))
    return (below + above) + (left + right)


def next_kernel(mine, shape_ref, outer_ref, inner_ref, pivot_ref, coupling_ref, offsets_ref,
                stiff_ref, right_ref, out_ref, values, low_rows, high_rows, spread):
    cells = pivot_ref.shape[0]
    even = lax.rem(mine[0], 2) == 0
    inner, outer = inner_ref[...].astype(F32), outer_ref[...].astype(F32)
    low_rows[...] = jnp.where(even, outer, inner)
    high_rows[...] = jnp.where(even, inner, outer)
    for k in range(cells):
        for c in range(3):
            row = 3 * k + c
            summed = around(
                shape_ref[k, c], low_rows[row : row + 1, :], high_rows[row : row + 1, :]
            )
            right_ref[k, c] = stiff_ref[k] * summed
    link = links_of(mine, coupling_ref, offsets_ref)
    local_ends(pivot_ref, link, right_ref, values, spread, out_ref)


def row_of(ref, row):
    return ref[row : row + 1, :]


def apply_map(maps_ref, base, vector):
    return [
        row_of(maps_ref, base + 3 * a) * vector[0]
        + row_of(maps_ref, base + 3 * a + 1) * vector[1]
        + row_of(maps_ref, base + 3 * a + 2) * vector[2]
        for a in range(3)
    ]


def chain(maps_ref, ends, wall, put):
    places = maps_ref.shape[0] // MAP_ROWS
    state = wall
    tops = []
    for place in range(places):
        base = place * MAP_ROWS
        end, top = ends(place)
        for c in range(3):
            put(place, c, state[c])
        reflected = apply_map(maps_ref, base + 18, state)
        tops.append([top[c] + reflected[c] for c in range(3)])
        moved = apply_map(maps_ref, base, state)
        state = [end[c] + moved[c] for c in range(3)]
    state = [jnp.zeros((1, LANES), F32)] * 3
    for place in range(places - 1, -1, -1):
        for c in range(3):
            put(place, 3 + c, state[c])
        moved = apply_map(maps_ref, place * MAP_ROWS + 9, state)
        state = [tops[place][c] + moved[c] for c in range(3)]


def first_chain_kernel(mine, maps_ref, mask_ref, keep_ref, got_ref, out_ref, wall_ref, sums, masks, flows):
    places = maps_ref.shape[0] // MAP_ROWS
    row, half = owned(mine)
    sums[...] = keep_ref[...] + got_ref[...]
    mask = mask_ref[...].astype(F32)
    masks[0, 8:16, :] = mask[:, :LANES]
    masks[1, 8:16, :] = mask[:, LANES:]
    masks[half, 7:8, :] = row_of(sums, 12)
    masks[half, 16:17, :] = row_of(sums, 13)
    low_mask = masks[half, pl.ds(7 + row, 1), :]
    own_mask = masks[half, pl.ds(8 + row, 1), :]
    high_mask = masks[half, pl.ds(9 + row, 1), :]
    other_mask = masks[1 - half, pl.ds(8 + row, 1), :]
    lane = lax.broadcasted_iota(jnp.int32, (1, LANES), 1)
    wall, around_wall = [], []
    for c in range(3):
        own = row_of(sums, 3 + c) * own_mask
        other = row_of(sums, 9 + c) * other_mask
        left_edge = jnp.where(half == 1, pltpu.roll(other, 1, 1), 0.0)
        right_edge = jnp.where(half == 0, pltpu.roll(other, LANES - 1, 1), 0.0)
        left = jnp.where(lane == 0, left_edge, pltpu.roll(own, 1, 1))
        right = jnp.where(lane == LANES - 1, right_edge, pltpu.roll(own, LANES - 1, 1))
        ends = row_of(sums, c) * low_mask + row_of(sums, 6 + c) * high_mask
        wall.append(own)
        around_wall.append(ends + (left + right))
        wall_ref[c : c + 1, :] = own

    def ends_at(place):
        base = place * MAP_ROWS
        return (
            apply_map(maps_ref, base + 27, around_wall),
            apply_map(maps_ref, base + 36, around_wall),
        )

    def put(place, c, value):
        row = place * FLOW_ROWS + 2 * c
        rounded = value.astype(jnp.bfloat16).astype(F32)
        flows[row : row + 1, :] = rounded
        flows[row + 1 : row + 2, :] = value - rounded

    chain(maps_ref, ends_at, wall, put)
    for place in range(places):
        row = place * FLOW_ROWS + 12
        for c in range(3):
            flows[row + c : row + c + 1, :] = around_wall[c]
        flows[row + 3 : row + 4, :] = jnp.zeros((1, LANES), F32)
    out_ref[...] = flows[...].astype(jnp.bfloat16)


def next_chain_kernel(mine, maps_ref, ends_ref, wall_ref, out_ref):
    def ends_at(place):
        base = place * END_ROWS
        return (
            [row_of(ends_ref, base + c) for c in range(3)],
            [row_of(ends_ref, base + 3 + c) for c in range(3)],
        )

    def put(place, c, value):
        out_ref[place * END_ROWS + c : place * END_ROWS + c + 1, :] = value

    chain(maps_ref, ends_at, [row_of(wall_ref, c) for c in range(3)], put)
    for place in range(ends_ref.shape[0] // END_ROWS):
        base = place * END_ROWS
        out_ref[base + 6 : base + 8, :] = jnp.zeros((2, LANES), F32)


def solve(mine, flow, right, pivot_ref, coupling_ref, offsets_ref, shape_ref, edges, values, done=None):
    cells = pivot_ref.shape[0]
    link = links_of(mine, coupling_ref, offsets_ref)
    state = [flow(c) for c in range(3)]
    for k in range(cells):
        here = link(k)
        given = right(k)
        state = product(pivot_ref, k, [given[b] + here * state[b] for b in range(3)])
        for b in range(3):
            values[k, b] = state[b]
    lifted = [flow(3 + c) for c in range(3)]
    for k in range(cells - 1, -1, -1):
        lifted = product(pivot_ref, k, lifted)
        state = [values[k, b] + lifted[b] for b in range(3)]
        for b in range(3):
            shape_ref[k, b] = state[b]
            if edges:
                row = 3 * k + b
                edges[2][row : row + 1, :] = state[b][0:1]
                edges[3][row : row + 1, :] = state[b][7:8]
        if done:
            done(k)
        if k:
            here = link(k)
            lifted = [here * v for v in state]
    if edges:
        even = lax.rem(mine[0], 2) == 0
        first, final = edges[2][...], edges[3][...]
        edges[0][...] = jnp.where(even, final, first).astype(jnp.bfloat16)
        edges[1][...] = jnp.where(even, first, final).astype(jnp.bfloat16)


def first_solve_kernel(depth, mine, flows_ref, stiff_ref, pivot_ref, coupling_ref, offsets_ref,
                       shape_ref, inner_ref, outer_ref, values, first_rows, last_rows, flows):
    cells = pivot_ref.shape[0]
    width = shape_ref.shape[3]
    flows[: flows_ref.shape[0], :] = flows_ref[...].astype(F32)
    around_wall = [get_lines(flows, 12 + c, FLOW_ROWS, width) for c in range(3)]

    def flow(c):
        return get_lines(flows, 2 * c, FLOW_ROWS, width) + get_lines(flows, 2 * c + 1, FLOW_ROWS, width)

    def right(k):
        weight = stiff_ref[k] * blend_of(depth, mine, cells, k)
        return [weight * v for v in around_wall]

    edges = (inner_ref, outer_ref, first_rows, last_rows)
    solve(mine, flow, right, pivot_ref, coupling_ref, offsets_ref, shape_ref, edges, values)


def solve_kernel(mine, flows_ref, right_ref, pivot_ref, coupling_ref, offsets_ref, shape_ref, *rest):
    spread, rest = rest[-1], rest[:-1]
    spread[: flows_ref.shape[0], :] = flows_ref[...]
    def right(k):
        return [right_ref[k, b] for b in range(3)]

    def flow(c):
        return get_lines(spread, c, END_ROWS, shape_ref.shape[3])

    local = (pivot_ref, coupling_ref, offsets_ref)
    if len(rest) > 3:
        edges = (rest[0], rest[1], rest[3], rest[4])
        solve(mine, flow, right, *local, shape_ref, edges, rest[2])
        return
    values, near, sent = rest
    pieces = [
        pltpu.make_async_copy(near.at[4 * i : 4 * i + 4], shape_ref.at[4 * i : 4 * i + 4], sent.at[i])
        for i in range(near.shape[0] // 4)
    ]

    def done(k):
        if k % 4 == 0:
            pieces[k // 4].start()

    solve(mine, flow, right, *local, near, (), values, done)
    for piece in pieces:
        piece.wait()


def per_device(
    mode_shapes,
    amplitude,
    mode_patch,
    column_patch,
    wall_mask,
    offsets,
    coupling,
    pivot_inv,
    stiffness,
):
    rows, width = wall_mask.shape
    cells = coupling.shape[0]
    surf, norm = lax.axis_size("surf"), lax.axis_size("norm")
    modes = jnp.transpose(mode_shapes, (0, 2, 1, 3))
    pivots = jnp.transpose(pivot_inv, (0, 2, 1, 3))
    cube = shaped(cells, 3, rows, width)
    scratch = pltpu.VMEM((cells, 3, rows, width), F32)
    edge = shaped(cells * 3, width, dtype=jnp.bfloat16)
    edge_scratch = pltpu.VMEM((cells * 3, width), F32)
    depth = cells * norm

    def swapped(block, axis, count):
        block = block.reshape((count, block.shape[0] // count) + block.shape[1:])
        block = lax.all_to_all(block, axis, 0, 0, tiled=True)
        return block.reshape((-1,) + block.shape[2:])

    def paired(part, bits):
        return lax.ppermute(part, "surf", [(i, i ^ bits) for i in range(surf)])

    size = surf * WALL_ROWS // 2
    given = (amplitude, mode_patch, modes, column_patch, wall_mask)
    keep, send, mask = call(
        wall_kernel,
        [shaped(size, LANES), shaped(size, LANES), shaped(rows, width, dtype=wall_mask.dtype)],
        [(pltpu.SMEM if a.ndim == 1 else pltpu.VMEM)(a.shape, a.dtype) for a in given]
        + [
            pltpu.VMEM((6, mode_shapes.shape[1] + 32, LANES), F32),
            pltpu.VMEM(((surf + 2) * WALL_STEP, LANES), F32),
            pltpu.SemaphoreType.DMA((5,)),
            pltpu.SemaphoreType.DMA((modes.shape[2] // 64,)),
        ],
        given,
        "walls",
        far=True,
    )
    got = paired(send, 1)
    (maps,) = call(
        functools.partial(maps_kernel, depth),
        [shaped(norm * MAP_ROWS, LANES)],
        [scratch, scratch, pltpu.VMEM(((norm + 1) * MAP_STEP, LANES), F32)],
        (pivots, coupling, offsets, stiffness),
        "maps",
    )
    maps, got = lax.optimization_barrier((maps, got))
    for shift in (3, 1):
        size //= 2
        keep, send = call(
            functools.partial(wall_sum_kernel, shift),
            [shaped(size, LANES)] * 2,
            [pltpu.VMEM((2 * size, LANES), F32)],
            (keep, got),
            "wall_sum",
        )
        got = paired(send, 1 << shift)
        if shift == 3:
            maps = swapped(maps, "norm", norm)
        size //= 2
        keep, send = call(wall_half_kernel, [shaped(size, LANES)] * 2, [], (keep, got), "wall_half")
        got = paired(send, 3 << shift)
    flows, wall = call(
        first_chain_kernel,
        [shaped(norm * FLOW_ROWS, LANES, dtype=jnp.bfloat16), shaped(8, LANES)],
        [
            pltpu.VMEM((WALL_ROWS, LANES), F32),
            pltpu.VMEM((2, 24, LANES), F32),
            pltpu.VMEM((norm * FLOW_ROWS, LANES), F32),
        ],
        (maps, mask, keep, got),
        "first_chain",
    )
    flows = swapped(flows, "norm", norm)
    local = (pivots, coupling, offsets)
    edges = [scratch, edge_scratch, edge_scratch]
    spread = pltpu.VMEM(((norm + 1) * END_ROWS, LANES), F32)
    shape, inner, outer = call(
        functools.partial(first_solve_kernel, depth),
        [cube, edge, edge],
        edges + [pltpu.VMEM(((norm + 1) * FLOW_ROWS, LANES), F32)],
        (flows, stiffness) + local,
        "first_solve",
    )
    for sweep in range(1, SWEEPS):
        outer = lax.ppermute(
            outer, "surf", [(i, (i - 1 + 2 * (i % 2)) % surf) for i in range(surf)]
        )
        inner = lax.ppermute(inner, "surf", [(i, i + 1 - 2 * (i % 2)) for i in range(surf)])
        right, ends = call(
            next_kernel,
            [cube, shaped(norm * END_ROWS, LANES)],
            edges + [spread],
                (shape, outer, inner) + local + (stiffness,),
            "next_ends",
        )
        ends = swapped(ends, "norm", norm)
        (flows,) = call(
            next_chain_kernel, [shaped(norm * END_ROWS, LANES)], [], (maps, ends, wall), "chain"
        )
        flows = swapped(flows, "norm", norm)
        last = sweep == SWEEPS - 1
        solved = call(
            solve_kernel,
            [cube] if last else [cube, edge, edge],
            ([scratch, scratch, pltpu.SemaphoreType.DMA((cells // 4,))] if last else edges) + [spread],
                (flows, right) + local,
            "solve",
            out_far=last,
        )
        if not last:
            shape, inner, outer = solved
    return jnp.transpose(solved[0], (0, 2, 1, 3))


def solution(mesh):
    return jax.shard_map(
        per_device,
        mesh=mesh,
        in_specs=(
            P("surf", None, None, None),
            P(),
            P(),
            P(),
            P("surf", None),
            P("surf", None),
            P("norm", "surf", None),
            P("norm", "surf", None, None),
            P("norm", "surf", None),
        ),
        out_specs=P("norm", "surf", None, None),
        check_vma=False,
    )
```

```python
import functools
import jax
import jax.numpy as jnp
from jax import lax
from jax.experimental import pallas as pl
from jax.experimental.pallas import tpu as pltpu
from jax.sharding import PartitionSpec as P

SWEEPS = 3
F32 = jnp.float32
LANES = 128
MAP_ROWS = 48
WALL_ROWS = 16
MAP_STEP = 56
WALL_STEP = 24
FLOW_ROWS = 16
END_ROWS = 8
VMEM_LIMIT = 16 * 1024 * 1024
VMEM_FRONT = 60 * 1024 * 1024


def call(kernel, outs, scratch, args, name, far=False, out_far=False):
    space = pltpu.HBM if far else pltpu.VMEM
    moved = sum(a.size * a.dtype.itemsize for a in list(args) + list(outs))

    def body(*refs):
        kernel((lax.axis_index("surf"), lax.axis_index("norm")), *refs)

    return pl.pallas_call(
        body,
        out_shape=outs,
        in_specs=[pl.BlockSpec(memory_space=space) for _ in args],
        out_specs=[pl.BlockSpec(memory_space=pltpu.HBM if out_far else pltpu.VMEM) for _ in outs],
        scratch_shapes=scratch,
        name=name,
        cost_estimate=pl.CostEstimate(flops=1000000, bytes_accessed=moved, transcendentals=0),
        compiler_params=pltpu.CompilerParams(vmem_limit_bytes=VMEM_FRONT if far else VMEM_LIMIT),
    )(*args)


def shaped(*shape, dtype=F32):
    return jax.ShapeDtypeStruct(shape, dtype)


def wall_parts(arrive, mine, amplitude_ref, patch_ref, modes_ref, columns_ref, mask_ref, keep_ref, send_ref, sums, blocks):
    own_modes = modes_ref.shape[0]
    count = modes_ref.shape[2]
    parts = 2 * keep_ref.shape[0] // WALL_ROWS
    base = mine[0] * own_modes
    row, half = owned(mine)

    def one(block, carry):
        rows = pl.ds(pl.multiple_of(block * 16, 16), 16)
        target = pl.ds(pl.multiple_of(block * 16 + 8, 8), 16)
        patch = columns_ref[rows, :]
        weights = [
            jnp.where(patch == patch_ref[base + m], amplitude_ref[base + m], 0.0)
            for m in range(own_modes)
        ]
        for c in range(3):
            total = weights[0] * modes_ref[0, c, rows, :].astype(F32)
            for m in range(1, own_modes):
                total = total + weights[m] * modes_ref[m, c, rows, :].astype(F32)
            sums[2 * c, target, :] = total[:, :LANES]
            sums[2 * c + 1, target, :] = total[:, LANES:]
        return carry

    for piece in range(count // 64):
        arrive(piece)
        lax.fori_loop(4 * piece, 4 * piece + 4, one, 0)
    for c in range(6):
        sums[c, 0:8, :] = sums[c, count : count + 8, :]
        sums[c, count + 8 : count + 16, :] = sums[c, 8:16, :]

    def put(place, from_ref, start):
        for odd in range(2):
            blocks[pl.ds(odd * (parts // 2) * WALL_STEP + place, parts // 2, stride=WALL_STEP), :] = (
                from_ref[pl.ds(start + 8 * odd, parts // 2, stride=16), :]
            )

    for c in range(3):
        for step in range(3):
            put(3 * step + c, sums.at[2 * c + half], 7 + row + step)
        put(9 + c, sums.at[2 * c + 1 - half], 8 + row)
    blank = jnp.zeros((parts, LANES), F32)
    for place in range(12, 16):
        blocks[pl.ds(place, parts, stride=WALL_STEP), :] = blank
    mask = jnp.where(half == 0, mask_ref[:, :LANES], mask_ref[:, LANES:]).astype(F32)
    for step, place, edge in ((1, 12, 7), (parts - 1, 13, 0)):
        target = lax.rem(mine[0] + step, parts)
        order = lax.rem(target, 2) * (parts // 2) + lax.div(target, 2)
        blocks[pl.ds(order * WALL_STEP + place, 1), :] = mask[edge : edge + 1]
    side = lax.rem(mine[0], 2)
    for ref, first in ((keep_ref, side), (send_ref, 1 - side)):
        for i in range(parts // 2):
            start = pl.multiple_of((first * (parts // 2) + i) * WALL_STEP, 8)
            ref[i * WALL_ROWS : (i + 1) * WALL_ROWS, :] = blocks[pl.ds(start, WALL_ROWS), :]


def wall_sum_kernel(shift, mine, keep_ref, got_ref, next_ref, send_ref, blocks):
    blocks[...] = keep_ref[...] + got_ref[...]
    rows = keep_ref.shape[0] // 4
    own = lax.rem(lax.shift_right_logical(mine[0], shift), 4)
    for ref, steps in ((next_ref, (0, 3)), (send_ref, (1, 2))):
        for i, step in enumerate(steps):
            start = pl.multiple_of(lax.bitwise_xor(own, step) * rows, 16)
            ref[i * rows : (i + 1) * rows, :] = blocks[pl.ds(start, rows), :]


def wall_half_kernel(mine, keep_ref, got_ref, next_ref, send_ref):
    rows = next_ref.shape[0]
    next_ref[...] = keep_ref[:rows] + got_ref[:rows]
    send_ref[...] = keep_ref[rows:] + got_ref[rows:]


def owned(mine):
    return lax.rem(mine[1], 8), lax.div(mine[1], 8)


def links_of(mine, coupling_ref, offsets_ref):
    cells = coupling_ref.shape[0]
    cut = offsets_ref[...] - mine[1] * cells

    def link(k):
        return jnp.where(cut == k, 0.0, coupling_ref[k])

    return link


def product(pivot_ref, k, vector):
    return [
        pivot_ref[k, 3 * a] * vector[0]
        + pivot_ref[k, 3 * a + 1] * vector[1]
        + pivot_ref[k, 3 * a + 2] * vector[2]
        for a in range(3)
    ]


def put_lines(out_ref, row, stride, value):
    for half in range(value.shape[1] // LANES):
        out_ref[pl.ds(half * 8 * stride + row, 8, stride=stride), :] = value[
            :, half * LANES : (half + 1) * LANES
        ]


def get_lines(in_ref, row, stride, width):
    return jnp.concatenate(
        [
            in_ref[pl.ds(half * 8 * stride + row, 8, stride=stride), :]
            for half in range(width // LANES)
        ],
        axis=1,
    )


def blend_of(depth, mine, cells, k):
    return 1.0 - (mine[1] * cells + k).astype(F32) * (1.0 / depth)


def maps_kernel(depth, mine, pivot_ref, coupling_ref, offsets_ref, stiff_ref, out_ref, prefix, driven, spread):
    cells = pivot_ref.shape[0]
    link = links_of(mine, coupling_ref, offsets_ref)
    first = link(0)

    def source(k, j):
        weight = stiff_ref[k] * blend_of(depth, mine, cells, k)
        return [pivot_ref[k, 3 * a + j] * weight for a in range(3)]

    for j in range(3):
        column = [pivot_ref[0, 3 * a + j] * first for a in range(3)]
        forced = source(0, j)
        for a in range(3):
            prefix[0, a] = column[a]
            driven[0, a] = forced[a]
        for k in range(1, cells):
            here = link(k)
            column = product(pivot_ref, k, [here * v for v in column])
            weight = stiff_ref[k] * blend_of(depth, mine, cells, k)
            forced = [here * v for v in forced]
            forced[j] = forced[j] + weight
            forced = product(pivot_ref, k, forced)
            for a in range(3):
                prefix[k, a] = column[a]
                driven[k, a] = forced[a]
        for a in range(3):
            put_lines(spread, 3 * a + j, MAP_STEP, column[a])
            put_lines(spread, 27 + 3 * a + j, MAP_STEP, forced[a])
        upper = [pivot_ref[cells - 1, 3 * a + j] for a in range(3)]
        for k in range(cells - 2, -1, -1):
            above = link(k + 1)
            column = product(pivot_ref, k, [above * v for v in column])
            column = [column[a] + prefix[k, a] for a in range(3)]
            forced = product(pivot_ref, k, [above * v for v in forced])
            forced = [forced[a] + driven[k, a] for a in range(3)]
            upper = product(pivot_ref, k, [above * v for v in upper])
        for a in range(3):
            put_lines(spread, 9 + 3 * a + j, MAP_STEP, first * upper[a])
            put_lines(spread, 18 + 3 * a + j, MAP_STEP, first * column[a])
            put_lines(spread, 36 + 3 * a + j, MAP_STEP, first * forced[a])
    blank = jnp.zeros_like(first)
    for a in range(45, MAP_ROWS):
        put_lines(spread, a, MAP_STEP, blank)
    for place in range(out_ref.shape[0] // MAP_ROWS):
        out_ref[place * MAP_ROWS : (place + 1) * MAP_ROWS, :] = spread[
            place * MAP_STEP : place * MAP_STEP + MAP_ROWS, :
        ]


def wall_kernel(mine, *rest):
    far, (keep_ref, send_ref, mask_ref), near = rest[:5], rest[5:8], rest[8:13]
    sums, blocks, arrived, pieces = rest[13:]
    modes = [
        pltpu.make_async_copy(
            far[2].at[:, :, 64 * i : 64 * (i + 1), :],
            near[2].at[:, :, 64 * i : 64 * (i + 1), :],
            pieces.at[i],
        )
        for i in range(near[2].shape[2] // 64)
    ]
    whole = [pltpu.make_async_copy(far[i], near[i], arrived.at[i]) for i in (0, 1, 3, 4)]
    for copy in whole + modes:
        copy.start()
    for copy in whole:
        copy.wait()
    mask_ref[...] = near[4][...]
    wall_parts(lambda i: modes[i].wait(), mine, *near, keep_ref, send_ref, sums, blocks)


def local_ends(pivot_ref, link, right_ref, values, spread, out_ref):
    cells = pivot_ref.shape[0]
    for k in range(cells):
        state = [right_ref[k, b] for b in range(3)] if k == 0 else [
            right_ref[k, b] + link(k) * state[b] for b in range(3)
        ]
        state = product(pivot_ref, k, state)
        for b in range(3):
            values[k, b] = state[b]
    for b in range(3):
        put_lines(spread, b, END_ROWS, state[b])
    for k in range(cells - 2, -1, -1):
        above = link(k + 1)
        lifted = product(pivot_ref, k, [above * v for v in state])
        state = [values[k, b] + lifted[b] for b in range(3)]
    first = link(0)
    for b in range(3):
        put_lines(spread, 3 + b, END_ROWS, first * state[b])
    blank = jnp.zeros_like(first)
    for b in range(6, END_ROWS):
        put_lines(spread, b, END_ROWS, blank)
    out_ref[...] = spread[: out_ref.shape[0], :]


def around(value, low, high):
    rows = lax.broadcasted_iota(jnp.int32, value.shape, 0)
    columns = lax.broadcasted_iota(jnp.int32, value.shape, 1)
    height, width = value.shape
    below = jnp.where(rows == 0, low, pltpu.roll(value, 1, 0))
    above = jnp.where(rows == height - 1, high, pltpu.roll(value, height - 1, 0))
    left = jnp.where(columns == 0, 0.0, pltpu.roll(value, 1, 1))
    right = jnp.where(columns == width - 1, 0.0, pltpu.roll(value, width - 1, 1))
    return (below + above) + (left + right)


def next_kernel(mine, shape_ref, outer_ref, inner_ref, pivot_ref, coupling_ref, offsets_ref,
                stiff_ref, right_ref, out_ref, values, low_rows, high_rows, spread):
    cells = pivot_ref.shape[0]
    even = lax.rem(mine[0], 2) == 0
    inner, outer = inner_ref[...].astype(F32), outer_ref[...].astype(F32)
    low_rows[...] = jnp.where(even, outer, inner)
    high_rows[...] = jnp.where(even, inner, outer)
    for k in range(cells):
        for c in range(3):
            row = 3 * k + c
            summed = around(
                shape_ref[k, c], low_rows[row : row + 1, :], high_rows[row : row + 1, :]
            )
            right_ref[k, c] = stiff_ref[k] * summed
    link = links_of(mine, coupling_ref, offsets_ref)
    local_ends(pivot_ref, link, right_ref, values, spread, out_ref)


def row_of(ref, row):
    return ref[row : row + 1, :]


def apply_map(maps_ref, base, vector):
    return [
        row_of(maps_ref, base + 3 * a) * vector[0]
        + row_of(maps_ref, base + 3 * a + 1) * vector[1]
        + row_of(maps_ref, base + 3 * a + 2) * vector[2]
        for a in range(3)
    ]


def chain(maps_ref, ends, wall, put):
    places = maps_ref.shape[0] // MAP_ROWS
    state = wall
    tops = []
    for place in range(places):
        base = place * MAP_ROWS
        end, top = ends(place)
        for c in range(3):
            put(place, c, state[c])
        reflected = apply_map(maps_ref, base + 18, state)
        tops.append([top[c] + reflected[c] for c in range(3)])
        moved = apply_map(maps_ref, base, state)
        state = [end[c] + moved[c] for c in range(3)]
    state = [jnp.zeros((1, LANES), F32)] * 3
    for place in range(places - 1, -1, -1):
        for c in range(3):
            put(place, 3 + c, state[c])
        moved = apply_map(maps_ref, place * MAP_ROWS + 9, state)
        state = [tops[place][c] + moved[c] for c in range(3)]


def first_chain_kernel(mine, maps_ref, mask_ref, keep_ref, got_ref, out_ref, wall_ref, sums, masks, flows):
    places = maps_ref.shape[0] // MAP_ROWS
    row, half = owned(mine)
    sums[...] = keep_ref[...] + got_ref[...]
    mask = mask_ref[...].astype(F32)
    masks[0, 8:16, :] = mask[:, :LANES]
    masks[1, 8:16, :] = mask[:, LANES:]
    masks[half, 7:8, :] = row_of(sums, 12)
    masks[half, 16:17, :] = row_of(sums, 13)
    low_mask = masks[half, pl.ds(7 + row, 1), :]
    own_mask = masks[half, pl.ds(8 + row, 1), :]
    high_mask = masks[half, pl.ds(9 + row, 1), :]
    other_mask = masks[1 - half, pl.ds(8 + row, 1), :]
    lane = lax.broadcasted_iota(jnp.int32, (1, LANES), 1)
    wall, around_wall = [], []
    for c in range(3):
        own = row_of(sums, 3 + c) * own_mask
        other = row_of(sums, 9 + c) * other_mask
        left_edge = jnp.where(half == 1, pltpu.roll(other, 1, 1), 0.0)
        right_edge = jnp.where(half == 0, pltpu.roll(other, LANES - 1, 1), 0.0)
        left = jnp.where(lane == 0, left_edge, pltpu.roll(own, 1, 1))
        right = jnp.where(lane == LANES - 1, right_edge, pltpu.roll(own, LANES - 1, 1))
        ends = row_of(sums, c) * low_mask + row_of(sums, 6 + c) * high_mask
        wall.append(own)
        around_wall.append(ends + (left + right))
        wall_ref[c : c + 1, :] = own

    def ends_at(place):
        base = place * MAP_ROWS
        return (
            apply_map(maps_ref, base + 27, around_wall),
            apply_map(maps_ref, base + 36, around_wall),
        )

    def put(place, c, value):
        row = place * FLOW_ROWS + 2 * c
        rounded = value.astype(jnp.bfloat16).astype(F32)
        flows[row : row + 1, :] = rounded
        flows[row + 1 : row + 2, :] = value - rounded

    chain(maps_ref, ends_at, wall, put)
    for place in range(places):
        row = place * FLOW_ROWS + 12
        for c in range(3):
            flows[row + c : row + c + 1, :] = around_wall[c]
        flows[row + 3 : row + 4, :] = jnp.zeros((1, LANES), F32)
    out_ref[...] = flows[...].astype(jnp.bfloat16)


def next_chain_kernel(mine, maps_ref, ends_ref, wall_ref, out_ref):
    def ends_at(place):
        base = place * END_ROWS
        return (
            [row_of(ends_ref, base + c) for c in range(3)],
            [row_of(ends_ref, base + 3 + c) for c in range(3)],
        )

    def put(place, c, value):
        out_ref[place * END_ROWS + c : place * END_ROWS + c + 1, :] = value

    chain(maps_ref, ends_at, [row_of(wall_ref, c) for c in range(3)], put)
    for place in range(ends_ref.shape[0] // END_ROWS):
        base = place * END_ROWS
        out_ref[base + 6 : base + 8, :] = jnp.zeros((2, LANES), F32)


def solve(mine, flow, right, pivot_ref, coupling_ref, offsets_ref, shape_ref, edges, values, done=None):
    cells = pivot_ref.shape[0]
    link = links_of(mine, coupling_ref, offsets_ref)
    state = [flow(c) for c in range(3)]
    for k in range(cells):
        here = link(k)
        given = right(k)
        state = product(pivot_ref, k, [given[b] + here * state[b] for b in range(3)])
        for b in range(3):
            values[k, b] = state[b]
    lifted = [flow(3 + c) for c in range(3)]
    for k in range(cells - 1, -1, -1):
        lifted = product(pivot_ref, k, lifted)
        state = [values[k, b] + lifted[b] for b in range(3)]
        for b in range(3):
            shape_ref[k, b] = state[b]
            if edges:
                row = 3 * k + b
                edges[2][row : row + 1, :] = state[b][0:1]
                edges[3][row : row + 1, :] = state[b][7:8]
        if done:
            done(k)
        if k:
            here = link(k)
            lifted = [here * v for v in state]
    if edges:
        even = lax.rem(mine[0], 2) == 0
        first, final = edges[2][...], edges[3][...]
        edges[0][...] = jnp.where(even, final, first).astype(jnp.bfloat16)
        edges[1][...] = jnp.where(even, first, final).astype(jnp.bfloat16)


def first_solve_kernel(depth, mine, flows_ref, stiff_ref, pivot_ref, coupling_ref, offsets_ref,
                       shape_ref, inner_ref, outer_ref, values, first_rows, last_rows, flows):
    cells = pivot_ref.shape[0]
    width = shape_ref.shape[3]
    flows[: flows_ref.shape[0], :] = flows_ref[...].astype(F32)
    around_wall = [get_lines(flows, 12 + c, FLOW_ROWS, width) for c in range(3)]

    def flow(c):
        return get_lines(flows, 2 * c, FLOW_ROWS, width) + get_lines(flows, 2 * c + 1, FLOW_ROWS, width)

    def right(k):
        weight = stiff_ref[k] * blend_of(depth, mine, cells, k)
        return [weight * v for v in around_wall]

    edges = (inner_ref, outer_ref, first_rows, last_rows)
    solve(mine, flow, right, pivot_ref, coupling_ref, offsets_ref, shape_ref, edges, values)


def solve_kernel(mine, flows_ref, right_ref, pivot_ref, coupling_ref, offsets_ref, shape_ref, *rest):
    spread, rest = rest[-1], rest[:-1]
    spread[: flows_ref.shape[0], :] = flows_ref[...]
    def right(k):
        return [right_ref[k, b] for b in range(3)]

    def flow(c):
        return get_lines(spread, c, END_ROWS, shape_ref.shape[3])

    local = (pivot_ref, coupling_ref, offsets_ref)
    if len(rest) > 3:
        edges = (rest[0], rest[1], rest[3], rest[4])
        solve(mine, flow, right, *local, shape_ref, edges, rest[2])
        return
    values, near, sent = rest
    pieces = [
        pltpu.make_async_copy(near.at[4 * i : 4 * i + 4], shape_ref.at[4 * i : 4 * i + 4], sent.at[i])
        for i in range(near.shape[0] // 4)
    ]

    def done(k):
        if k % 4 == 0:
            pieces[k // 4].start()

    solve(mine, flow, right, *local, near, (), values, done)
    for piece in pieces:
        piece.wait()


def per_device(
    mode_shapes,
    amplitude,
    mode_patch,
    column_patch,
    wall_mask,
    offsets,
    coupling,
    pivot_inv,
    stiffness,
):
    rows, width = wall_mask.shape
    cells = coupling.shape[0]
    surf, norm = lax.axis_size("surf"), lax.axis_size("norm")
    modes = jnp.transpose(mode_shapes, (0, 2, 1, 3))
    pivots = jnp.transpose(pivot_inv, (0, 2, 1, 3))
    cube = shaped(cells, 3, rows, width)
    scratch = pltpu.VMEM((cells, 3, rows, width), F32)
    edge = shaped(cells * 3, width, dtype=jnp.bfloat16)
    edge_scratch = pltpu.VMEM((cells * 3, width), F32)
    depth = cells * norm

    def swapped(block, axis, count):
        block = block.reshape((count, block.shape[0] // count) + block.shape[1:])
        block = lax.all_to_all(block, axis, 0, 0, tiled=True)
        return block.reshape((-1,) + block.shape[2:])

    def paired(part, bits):
        return lax.ppermute(part, "surf", [(i, i ^ bits) for i in range(surf)])

    size = surf * WALL_ROWS // 2
    given = (amplitude, mode_patch, modes, column_patch, wall_mask)
    keep, send, mask = call(
        wall_kernel,
        [shaped(size, LANES), shaped(size, LANES), shaped(rows, width, dtype=wall_mask.dtype)],
        [(pltpu.SMEM if a.ndim == 1 else pltpu.VMEM)(a.shape, a.dtype) for a in given]
        + [
            pltpu.VMEM((6, mode_shapes.shape[1] + 32, LANES), F32),
            pltpu.VMEM(((surf + 2) * WALL_STEP, LANES), F32),
            pltpu.SemaphoreType.DMA((5,)),
            pltpu.SemaphoreType.DMA((modes.shape[2] // 64,)),
        ],
        given,
        "walls",
        far=True,
    )
    got = paired(send, 1)
    (maps,) = call(
        functools.partial(maps_kernel, depth),
        [shaped(norm * MAP_ROWS, LANES)],
        [scratch, scratch, pltpu.VMEM(((norm + 1) * MAP_STEP, LANES), F32)],
        (pivots, coupling, offsets, stiffness),
        "maps",
    )
    maps, got = lax.optimization_barrier((maps, got))
    for shift in (3, 1):
        size //= 2
        keep, send = call(
            functools.partial(wall_sum_kernel, shift),
            [shaped(size, LANES)] * 2,
            [pltpu.VMEM((2 * size, LANES), F32)],
            (keep, got),
            "wall_sum",
        )
        got = paired(send, 1 << shift)
        if shift == 3:
            maps = swapped(maps, "norm", norm)
        size //= 2
        keep, send = call(wall_half_kernel, [shaped(size, LANES)] * 2, [], (keep, got), "wall_half")
        got = paired(send, 3 << shift)
    flows, wall = call(
        first_chain_kernel,
        [shaped(norm * FLOW_ROWS, LANES, dtype=jnp.bfloat16), shaped(8, LANES)],
        [
            pltpu.VMEM((WALL_ROWS, LANES), F32),
            pltpu.VMEM((2, 24, LANES), F32),
            pltpu.VMEM((norm * FLOW_ROWS, LANES), F32),
        ],
        (maps, mask, keep, got),
        "first_chain",
    )
    flows = swapped(flows, "norm", norm)
    local = (pivots, coupling, offsets)
    edges = [scratch, edge_scratch, edge_scratch]
    spread = pltpu.VMEM(((norm + 1) * END_ROWS, LANES), F32)
    shape, inner, outer = call(
        functools.partial(first_solve_kernel, depth),
        [cube, edge, edge],
        edges + [pltpu.VMEM(((norm + 1) * FLOW_ROWS, LANES), F32)],
        (flows, stiffness) + local,
        "first_solve",
    )
    for sweep in range(1, SWEEPS):
        outer = lax.ppermute(
            outer, "surf", [(i, (i - 1 + 2 * (i % 2)) % surf) for i in range(surf)]
        )
        inner = lax.ppermute(inner, "surf", [(i, i + 1 - 2 * (i % 2)) for i in range(surf)])
        right, ends = call(
            next_kernel,
            [cube, shaped(norm * END_ROWS, LANES)],
            edges + [spread],
                (shape, outer, inner) + local + (stiffness,),
            "next_ends",
        )
        ends = swapped(ends, "norm", norm)
        (flows,) = call(
            next_chain_kernel, [shaped(norm * END_ROWS, LANES)], [], (maps, ends, wall), "chain"
        )
        flows = swapped(flows, "norm", norm)
        last = sweep == SWEEPS - 1
        solved = call(
            solve_kernel,
            [cube] if last else [cube, edge, edge],
            ([scratch, scratch, pltpu.SemaphoreType.DMA((cells // 4,))] if last else edges) + [spread],
                (flows, right) + local,
            "solve",
            out_far=last,
        )
        if not last:
            shape, inner, outer = solved
    return jnp.transpose(solved[0], (0, 2, 1, 3))


def solution(mesh):
    return jax.shard_map(
        per_device,
        mesh=mesh,
        in_specs=(
            P("surf", None, None, None),
            P(),
            P(),
            P(),
            P("surf", None),
            P("surf", None),
            P("norm", "surf", None),
            P("norm", "surf", None, None),
            P("norm", "surf", None),
        ),
        out_specs=P("norm", "surf", None, None),
        check_vma=False,
    )
```
